128 devices in a mesh: feat: 16 (over z, y), batch: 8 (over x, core).
Axes of the slice: x: 4, y: 4, z: 4, core: 2. Of those that a mesh axis runs over, the one named last changes fastest.
Arguments:
- features: bfloat16 [768, 131072], P('feat', 'batch'), may hold values from -6 to 6
- sampled_slots: int32 [8, 8, 16, 4096], P(None, 'batch'), may hold values from 0 to 2047
- block_index: int32 [8, 8, 32, 16], P(None, 'batch'), may hold values from 0 to 127
- counts: int32 [8, 8, 4096], replicated, may hold values from 1 to 16
- weight: bfloat16 [768, 1024], P('feat'), may hold values from -1.75 to 1.75
- cotangent: bfloat16 [32768, 1024], P(('feat', 'batch')), may hold values from -0.59765625 to 0.59765625
Outputs:
- hidden: bfloat16 [32768, 1024], P(('feat', 'batch'))
- weight_grad: float32 [768, 1024], P('feat')
The draws below stay inside these ranges and needn't reach their ends.
Inputs may be any that keep to these rules, and one draw needn't show every extreme that they name: A stored value v = sampled_slots[g, p, s, j] names entry v // 128 of block_index's list for block j // 128, and node v % 128 of that tile.
All inputs are finite; a program needn't handle non-finite values.
Results may differ from the reference program's by a relative error of at most 0.0053.
Values may be sent and summed in bfloat16 or wider, within the bound.
A program may use at most 128 MiB of HBM per device.

```python
import jax
import jax.numpy as jnp
from jax import lax

D = 768
H = 1024
ROWS_DEV = 256
NODES_DEV = 16384
FANOUT = 16
TILES = 16
GROUPS = 8
GROUP_ROWS = 4096
ROW_BLOCKS = 32
ROWS = 32768
NODES = 131072
NODE_BLOCKS = 128
N_FEAT = 16


def with_ends(array, stream_key, low, high):
    spot = [jax.random.randint(jax.random.fold_in(stream_key, axis), (), 0, length) for axis, length in enumerate(array.shape)]
    widest = array.shape.index(max(array.shape))
    neighbour = spot[:widest] + [(spot[widest] + 1) % array.shape[widest]] + spot[widest + 1:]
    return array.at[tuple(spot)].set(low).at[tuple(neighbour)].set(high)


def level_of(key, shape, pieces, least, largest):
    loudness = 1.0
    for axis_at, parts in pieces:
        steps = jax.random.uniform(jax.random.fold_in(jax.random.fold_in(key, 6), axis_at), (parts,), jnp.float32, least / len(pieces), largest / len(pieces))
        loudness = loudness * jnp.repeat(jnp.exp(steps), shape[axis_at] // parts).reshape((-1,) + (1,) * (len(shape) - 1 - axis_at))
    return loudness


def normal_values(own_key, extent, deviation, limit, cuts=(), kind=jnp.bfloat16):
    values = jax.random.normal(own_key, extent, jnp.float32) * deviation
    if len(cuts) > 0:
        values = level_of(own_key, extent, cuts, -0.22, 0.18) * values
    return jnp.clip(values, min=-limit, max=limit).astype(kind)


def setup_inputs(seed: int = 0) -> dict:
    arg_keys = jax.random.split(jax.random.key(seed), 7)
    return {
        "features": normal_values(arg_keys[0], (D, NODES), 1.0, 6.0, ((0, 16), (1, 8))),
        "sampled_slots": with_ends(jax.random.randint(arg_keys[1], (GROUPS, GROUPS, FANOUT, GROUP_ROWS), 0, TILES * 128), jax.random.fold_in(arg_keys[1], 1), 0, (TILES * 128) - 1).astype(jnp.int32),
        "block_index": with_ends(jax.random.randint(arg_keys[2], (GROUPS, GROUPS, ROW_BLOCKS, TILES), 0, NODE_BLOCKS), jax.random.fold_in(arg_keys[2], 1), 0, NODE_BLOCKS - 1).astype(jnp.int32),
        "counts": with_ends(jax.random.randint(arg_keys[3], (GROUPS, GROUPS, GROUP_ROWS), 1, FANOUT + 1), jax.random.fold_in(arg_keys[3], 1), 1, FANOUT).astype(jnp.int32),
        "weight": normal_values(arg_keys[4], (D, H), (D // 64) ** -0.5, 1.75, ((0, 16),)),
        "cotangent": normal_values(arg_keys[5], (ROWS, H), 0.1, 0.59765625, ((0, 128),)),
    }


def reference(features, sampled_slots, block_index, counts, weight, cotangent):
    node_rows = features.T
    row_block = jnp.arange(GROUP_ROWS, dtype=jnp.int32) // 128
    slot_order = jnp.arange(FANOUT, dtype=jnp.int32)

    def one_group(group_id):
        def add_part(running, part_id):
            chosen = sampled_slots[group_id, part_id]
            tile_list = block_index[group_id, part_id]
            tile_ids = tile_list[row_block[None, :], chosen // 128]
            node_ids = (part_id * NODES_DEV + tile_ids * 128 + chosen % 128).astype(jnp.int32)
            live_mask = (slot_order[:, None] < counts[group_id, part_id][None, :]).astype(jnp.float32)

            def add_slot(inner, slot_id):
                picked = node_rows[node_ids[slot_id]].astype(jnp.float32)
                return inner + live_mask[slot_id][:, None] * picked, None

            running, unused = lax.scan(add_slot, running, jnp.arange(FANOUT, dtype=jnp.int32))
            return running, None

        start_sum = jnp.zeros((GROUP_ROWS, D), jnp.float32)
        summed, unused = lax.scan(add_part, start_sum, jnp.arange(GROUPS, dtype=jnp.int32))
        totals = jnp.sum(counts[group_id], axis=0).astype(jnp.float32)
        return (summed / totals[:, None]).astype(jnp.bfloat16)

    grouped = lax.map(one_group, jnp.arange(GROUPS, dtype=jnp.int32))
    aggregate = grouped.reshape(GROUPS, N_FEAT, ROWS_DEV, D).transpose(1, 0, 2, 3).reshape(ROWS, D)
    preact = jnp.dot(aggregate, weight, preferred_element_type=jnp.float32)
    sigmoid_val = jax.nn.sigmoid(preact)
    hidden = (preact * sigmoid_val).astype(jnp.bfloat16)
    pre_grad = (cotangent.astype(jnp.float32) * sigmoid_val * (1.0 + preact * (1.0 - sigmoid_val))).astype(jnp.bfloat16)
    weight_grad = jnp.dot(aggregate.T, pre_grad, preferred_element_type=jnp.float32)
    return hidden, weight_grad
```

```python
import jax
import jax.numpy as jnp
from jax import lax
from jax.experimental import pallas as pl
from jax.experimental.pallas import tpu as pltpu
from jax.sharding import PartitionSpec as P

BF = jnp.bfloat16
F32 = jnp.float32
NT = (((1,), (1,)), ((), ()))


def shift(array, axis, move):
    size = lax.axis_size(axis)
    return lax.ppermute(array, axis, [(at, move(at)) for at in range(size)])


def along_z(array, step):
    return shift(array, "feat", lambda at: (at + 4 * step) % 16)


def along_y(array, step):
    return shift(array, "feat", lambda at: at // 4 * 4 + (at + step) % 4)


def along_x(array, step):
    return shift(array, "batch", lambda at: (at + 2 * step) % 8)


def flip(array, bit):
    return shift(array, "batch", lambda at: at ^ bit)


def edge_codes(slots, used):
    slot_row = lax.broadcasted_iota(jnp.int32, slots.shape, 0) & 15
    lane = lax.broadcasted_iota(jnp.int32, slots.shape, 1)
    height = slots.shape[0]
    value = jnp.where(slot_row < used, slots, -1)
    for bit in range(4):
        rows, lanes = 1 << bit, 8 << bit
        row_bit = (slot_row >> bit) & 1
        lane_bit = (lane >> (bit + 3)) & 1
        later = pltpu.roll(pltpu.roll(value, height - rows, 0), lanes, 1)
        earlier = pltpu.roll(pltpu.roll(value, rows, 0), 128 - lanes, 1)
        value = jnp.where(row_bit < lane_bit, later, jnp.where(row_bit > lane_bit, earlier, value))
    return (value >> 7) * 8 + (lane & 7), value & 127


def onehot(code):
    rows = lax.broadcasted_iota(jnp.int32, (128, 128), 0).astype(BF)
    match = jnp.broadcast_to(code.astype(BF), (128, 128)) == rows
    return jnp.where(match, BF(1), BF(0))


def group_at(step, where):
    other = 1 - step // 4
    return lax.rem(where[0] + step % 4, 4) * 2 + lax.rem(where[1] + other, 2)


def sum_kernel(where, tiles, slots, counts, f0, f1, f2, f3, out, tile_codes, node_codes, adjacency):
    group = group_at(pl.program_id(0), where)
    part = where[0] * 2 + where[1]
    used = counts[0, pl.ds(part, 1), :]
    tile_code, node_code = edge_codes(
        jnp.concatenate([slots[0, 0, :, b * 128:b * 128 + 128] for b in range(8)], 0),
        jnp.concatenate([jnp.broadcast_to(used[:, b * 128:b * 128 + 128], (16, 128)) for b in range(8)], 0),
    )
    tile_codes[...] = tile_code
    node_codes[...] = node_code

    def build(block, slot):
        blank = jnp.zeros((128, 128), BF)
        for pair in range(8):
            row = block * 16 + 2 * pair
            tile_a, tile_b = onehot(tile_codes[pl.ds(row, 1)]), onehot(tile_codes[pl.ds(row + 1, 1)])
            node_a, node_b = onehot(node_codes[pl.ds(row, 1)]), onehot(node_codes[pl.ds(row + 1, 1)])
            both = lax.dot_general(
                jnp.concatenate([tile_a, tile_b], 1),
                jnp.concatenate([jnp.concatenate([node_a, blank], 1), jnp.concatenate([blank, node_b], 1)], 0),
                NT,
                preferred_element_type=F32,
            )
            rows = jnp.concatenate([both[:, :128].reshape(16, 8, 128), both[:, 128:].reshape(16, 8, 128)], 1).astype(BF)
            for tile in range(16):
                adjacency[slot, tile // 2, pair * 16:pair * 16 + 16, tile % 2 * 128:tile % 2 * 128 + 128] = rows[tile]

    def multiply(block, slot):
        total = jnp.zeros((192, 128), F32)
        for pair in range(8):
            entry = group * 512 + (where[2] * 8 + block) * 16 + pair * 2
            halves = []
            for half in range(2):
                start = pl.multiple_of(tiles[entry + half] * 128, 128)
                halves.append(jnp.concatenate([ref[:, pl.ds(start, 128)] for ref in (f0, f1, f2, f3)], 0))
            total += lax.dot_general(jnp.concatenate(halves, 1), adjacency[slot, pair], NT, preferred_element_type=F32)
        out[0, :, pl.ds(pl.multiple_of(block * 128, 128), 128)] = total.astype(BF)

    def body(turn, unused):
        for at in range(4):
            build(turn * 4 + at, at)
        for at in range(4):
            multiply(turn * 4 + at, at)
        return 0

    lax.fori_loop(0, 2, body, 0)


def neighbour_sums(where, tiles, slots, counts, feats):
    whole = pl.BlockSpec((48, 16384), lambda i, where, tiles: (0, 0))
    return pl.pallas_call(
        sum_kernel,
        grid_spec=pltpu.PrefetchScalarGridSpec(
            num_scalar_prefetch=2,
            grid=(8,),
            in_specs=[
                pl.BlockSpec((1, 1, 16, 1024), lambda i, where, tiles: (group_at(i, where), 0, 0, where[2])),
                pl.BlockSpec((1, 8, 1024), lambda i, where, tiles: (group_at(i, where), 0, where[2])),
                whole, whole, whole, whole,
            ],
            out_specs=pl.BlockSpec((1, 192, 1024), lambda i, where, tiles: (i, 0, 0)),
            scratch_shapes=[
                pltpu.VMEM((128, 128), jnp.int32),
                pltpu.VMEM((128, 128), jnp.int32),
                pltpu.VMEM((4, 8, 128, 256), BF),
            ],
        ),
        out_shape=jax.ShapeDtypeStruct((8, 192, 1024), BF),
        compiler_params=pltpu.CompilerParams(vmem_limit_bytes=48 << 20),
    )(where, tiles, slots, counts, *feats)


def per_device(features, sampled_slots, block_index, counts, weight, cotangent):
    feat, batch = lax.axis_index("feat"), lax.axis_index("batch")
    z, y, x, core = feat // 4, feat % 4, batch // 2, batch % 2
    where = jnp.stack([x, core, z]).astype(jnp.int32)

    def around_z(array):
        return [array] + [along_z(array, -step) for step in (1, 2, 3)]

    sums = neighbour_sums(where, block_index.reshape(-1), sampled_slots, counts, around_z(features))
    mine = sums[4:].astype(F32) + flip(sums[:4], 1).astype(F32)
    mine_bf = mine.astype(BF)
    summed = mine[0]
    for step in (1, 2, 3):
        summed = summed + along_x(mine_bf[step], step).astype(F32)
    own_counts = lax.dynamic_slice(counts, (batch, 0, z * 1024), (1, 8, 1024))[0]
    totals = jnp.sum(own_counts, axis=0).astype(F32)
    aggregate = (summed / totals[None, :]).astype(BF)
    weights = jnp.concatenate(around_z(weight), 0)

    def rows_of(step):
        return lax.dynamic_slice(aggregate, (0, (y + step) % 4 * 256), (192, 256))

    rows = [rows_of(step) for step in range(4)]
    parts = [jnp.einsum("dr,dh->rh", block, weights, preferred_element_type=F32) for block in rows]
    preact = parts[0]
    for step in (1, 2, 3):
        preact = preact + along_y(parts[step].astype(BF), step).astype(F32)
    sigmoid_val = jax.nn.sigmoid(preact)
    hidden = (preact * sigmoid_val).astype(BF)
    pre_grad = (cotangent.astype(F32) * sigmoid_val * (1.0 + preact * (1.0 - sigmoid_val))).astype(BF)
    grad = jnp.dot(rows[0], pre_grad, preferred_element_type=F32)
    for step in (1, 2, 3):
        grad = grad + jnp.dot(rows[step], along_y(pre_grad, -step), preferred_element_type=F32)
    grad = grad.reshape(4, 48, 1024)
    weight_grad = grad[0]
    for step in (1, 2, 3):
        weight_grad = weight_grad + along_z(grad[step], step)
    for bit in (1, 2, 4):
        weight_grad = weight_grad + flip(weight_grad, bit)
    return hidden, weight_grad


def solution(mesh):
    placed = (
        P("feat", "batch"),
        P(None, "batch", None, None),
        P(None, "batch", None, None),
        P(),
        P("feat", None),
        P(("feat", "batch"), None),
    )
    return jax.shard_map(
        per_device,
        mesh=mesh,
        in_specs=placed,
        out_specs=(P(("feat", "batch"), None), P("feat", None)),
        check_vma=False,
    )
```

```python
import jax
import jax.numpy as jnp
from jax import lax
from jax.experimental import pallas as pl
from jax.experimental.pallas import tpu as pltpu
from jax.sharding import PartitionSpec as P

BF = jnp.bfloat16
F32 = jnp.float32
NT = (((1,), (1,)), ((), ()))


def shift(array, axis, move):
    size = lax.axis_size(axis)
    return lax.ppermute(array, axis, [(at, move(at)) for at in range(size)])


def along_z(array, step):
    return shift(array, "feat", lambda at: (at + 4 * step) % 16)


def along_y(array, step):
    return shift(array, "feat", lambda at: at // 4 * 4 + (at + step) % 4)


def flip(array, bit):
    return shift(array, "batch", lambda at: at ^ bit)


def edge_codes(slots, used):
    slot_row = lax.broadcasted_iota(jnp.int32, slots.shape, 0) & 15
    lane = lax.broadcasted_iota(jnp.int32, slots.shape, 1)
    height = slots.shape[0]
    value = jnp.where(slot_row < used, slots, -1)
    for bit in range(4):
        rows, lanes = 1 << bit, 8 << bit
        row_bit = (slot_row >> bit) & 1
        lane_bit = (lane >> (bit + 3)) & 1
        later = pltpu.roll(pltpu.roll(value, height - rows, 0), lanes, 1)
        earlier = pltpu.roll(pltpu.roll(value, rows, 0), 128 - lanes, 1)
        value = jnp.where(row_bit < lane_bit, later, jnp.where(row_bit > lane_bit, earlier, value))
    return (value >> 7) * 8 + (lane & 7), value & 127


def onehot(code):
    rows = lax.broadcasted_iota(jnp.int32, (128, 128), 0).astype(BF)
    match = jnp.broadcast_to(code.astype(BF), (128, 128)) == rows
    return jnp.where(match, BF(1), BF(0))


def group_at(step, where):
    return lax.rem(where[0] + 3 - step % 4, 4) * 2 + lax.rem(where[1] + 1 - step // 4, 2)


def build(adjacency, pairs_at, block, tile_codes, node_codes):
    blank = jnp.zeros((128, 128), BF)
    for pair in range(8):
        row = block * 16 + 2 * pair
        tile_a, tile_b = onehot(tile_codes[pl.ds(row, 1)]), onehot(tile_codes[pl.ds(row + 1, 1)])
        node_a, node_b = onehot(node_codes[pl.ds(row, 1)]), onehot(node_codes[pl.ds(row + 1, 1)])
        both = lax.dot_general(
            jnp.concatenate([tile_a, tile_b], 1),
            jnp.concatenate([jnp.concatenate([node_a, blank], 1), jnp.concatenate([blank, node_b], 1)], 0),
            NT,
            preferred_element_type=F32,
        )
        rows = jnp.concatenate([both[:, :128].reshape(16, 8, 128), both[:, 128:].reshape(16, 8, 128)], 1).astype(BF)
        for tile in range(16):
            adjacency[pairs_at, tile // 2, pair * 16:pair * 16 + 16, tile % 2 * 128:tile % 2 * 128 + 128] = rows[tile]


def remote(src, dst, sems, at, target):
    return pltpu.make_async_remote_copy(
        src_ref=src, dst_ref=dst, send_sem=sems.at[0, at], recv_sem=sems.at[1, at],
        device_id=target, device_id_type=pl.DeviceIdType.MESH,
    )


def sum_kernel(
    features, slots, counts, tiles, aggregate,
    raw, feats, slot_rows, used, tile_codes, node_codes, adjacency, core_out, core_in, x_out, x_in, own,
    load_sems, z_sems, core_sems, x_sems,
):
    feat, batch = lax.axis_index("feat"), lax.axis_index("batch")
    z, y, x, core = feat // 4, feat % 4, batch // 2, batch % 2
    where = (x, core)

    def z_at(step):
        return (lax.rem(z + step, 4) * 4 + y, batch)

    def x_at(step):
        return (feat, lax.rem(x + step, 4) * 2 + core)

    partner = (feat, x * 2 + 1 - core)
    barrier = pltpu.get_barrier_semaphore()
    for device in (z_at(1), z_at(3), partner, x_at(1), x_at(2), x_at(3)):
        pl.semaphore_signal(barrier, inc=1, device_id=device, device_id_type=pl.DeviceIdType.MESH)
    own_columns = pl.ds(pl.multiple_of(z * 1024, 1024), 1024)
    loads = [
        pltpu.make_async_copy(slots.at[:, 0, :, own_columns], slot_rows, load_sems.at[0]),
        pltpu.make_async_copy(counts.at[:, :, own_columns], used, load_sems.at[1]),
        pltpu.make_async_copy(features, raw, load_sems.at[2]),
    ]
    for load in loads:
        load.start()
    loads[2].wait()
    for tile in range(128):
        feats[tile, 0:48, :] = raw[:, tile * 128:tile * 128 + 128]
    pl.semaphore_wait(barrier, 6)

    low, high = pl.ds(0, 64), pl.ds(64, 64)

    def shard(at, tiles_of):
        return feats.at[tiles_of, pl.ds(48 * at, 48), :]

    ring = [
        remote(shard(0, low), shard(3, low), z_sems, 0, z_at(1)),
        remote(shard(0, high), shard(1, high), z_sems, 1, z_at(3)),
        remote(shard(0, high), shard(3, high), z_sems, 2, z_at(1)),
        remote(shard(0, low), shard(1, low), z_sems, 3, z_at(3)),
        remote(shard(3, low), shard(2, low), z_sems, 4, z_at(1)),
        remote(shard(1, high), shard(2, high), z_sems, 5, z_at(3)),
    ]
    ring[0].start()
    ring[1].start()
    loads[0].wait()
    loads[1].wait()

    def build_group(step, unused):
        group = group_at(step, where)
        group_used = used[group, pl.ds(batch, 1), :]
        tile_code, node_code = edge_codes(
            jnp.concatenate([slot_rows[group, :, b * 128:b * 128 + 128] for b in range(8)], 0),
            jnp.concatenate([jnp.broadcast_to(group_used[:, b * 128:b * 128 + 128], (16, 128)) for b in range(8)], 0),
        )
        tile_codes[...] = tile_code
        node_codes[...] = node_code

        def some(turn, unused):
            for at in range(4):
                build(adjacency, step * 8 + turn * 4 + at, turn * 4 + at, tile_codes, node_codes)
            return 0

        return lax.fori_loop(0, 2, some, 0)

    lax.fori_loop(0, 4, build_group, 0)
    ring[2].start()
    ring[3].start()
    lax.fori_loop(4, 6, build_group, 0)
    ring[0].wait_recv()
    ring[1].wait_recv()
    ring[4].start()
    ring[5].start()
    lax.fori_loop(6, 8, build_group, 0)
    for at in (2, 3, 4, 5):
        ring[at].wait_recv()
    for at in range(6):
        ring[at].wait_send()

    def products(step, put):
        group = group_at(step, where)

        def one(block):
            total = jnp.zeros((192, 128), F32)
            for pair in range(8):
                entry = (z * 8 + block) * 16 + pair * 2
                halves = [feats[tiles[group, entry + half]] for half in range(2)]
                total += lax.dot_general(
                    jnp.concatenate(halves, 1), adjacency[step * 8 + block, pair], NT, preferred_element_type=F32
                )
            put(pl.ds(pl.multiple_of(block * 128, 128), 128), total)

        def some(turn, unused):
            for at in range(4):
                one(turn * 4 + at)
            return 0

        lax.fori_loop(0, 2, some, 0)

    def core_copy(at):
        return remote(core_out.at[at], core_in.at[at], core_sems, at, partner)

    def x_copy(at):
        return remote(x_out.at[at], x_in.at[at], x_sems, at, x_at(3 - at))

    def for_partner(step, unused):
        def put(columns, total):
            core_out[step, :, columns] = total

        products(step, put)
        core_copy(step).start()
        return 0

    lax.fori_loop(0, 4, for_partner, 0)

    def for_x(at, unused):
        core_copy(at).wait_recv()

        def put(columns, total):
            x_out[at, :, columns] = (total + core_in[at, :, columns]).astype(BF)

        products(at + 4, put)
        x_copy(at).start()
        return 0

    lax.fori_loop(0, 3, for_x, 0)
    core_copy(3).wait_recv()

    def put_own(columns, total):
        own[:, columns] = total + core_in[3, :, columns]

    products(7, put_own)
    totals = jnp.sum(used[batch], axis=0, keepdims=True).astype(F32)
    for at in range(3):
        x_copy(at).wait_recv()
    for block in range(8):
        columns = slice(block * 128, block * 128 + 128)
        summed = own[:, columns]
        for at in range(3):
            summed = summed + x_in[at, :, columns].astype(F32)
        aggregate[:, columns] = (summed / totals[:, columns]).astype(BF)
    for at in range(4):
        core_copy(at).wait_send()
    for at in range(3):
        x_copy(at).wait_send()


def neighbour_sums(features, slots, counts, tiles):
    hbm = pl.BlockSpec(memory_space=pl.ANY)
    return pl.pallas_call(
        sum_kernel,
        in_specs=[hbm, hbm, hbm, pl.BlockSpec(memory_space=pltpu.SMEM)],
        out_specs=pl.BlockSpec(memory_space=pltpu.VMEM),
        scratch_shapes=[
            pltpu.VMEM((48, 16384), BF),
            pltpu.VMEM((128, 192, 128), BF),
            pltpu.VMEM((8, 16, 1024), jnp.int32),
            pltpu.VMEM((8, 8, 1024), jnp.int32),
            pltpu.VMEM((128, 128), jnp.int32),
            pltpu.VMEM((128, 128), jnp.int32),
            pltpu.VMEM((64, 8, 128, 256), BF),
            pltpu.VMEM((4, 192, 1024), F32),
            pltpu.VMEM((4, 192, 1024), F32),
            pltpu.VMEM((3, 192, 1024), BF),
            pltpu.VMEM((3, 192, 1024), BF),
            pltpu.VMEM((192, 1024), F32),
            pltpu.SemaphoreType.DMA((3,)),
            pltpu.SemaphoreType.DMA((2, 6)),
            pltpu.SemaphoreType.DMA((2, 4)),
            pltpu.SemaphoreType.DMA((2, 3)),
        ],
        out_shape=jax.ShapeDtypeStruct((192, 1024), BF),
        compiler_params=pltpu.CompilerParams(vmem_limit_bytes=60 << 20, collective_id=0, has_side_effects=True),
    )(features, slots, counts, tiles)


def per_device(features, sampled_slots, block_index, counts, weight, cotangent):
    feat, batch = lax.axis_index("feat"), lax.axis_index("batch")
    z, y, x, core = feat // 4, feat % 4, batch // 2, batch % 2

    def around_z(array):
        return [array] + [along_z(array, -step) for step in (1, 2, 3)]

    aggregate = neighbour_sums(features, sampled_slots, counts, block_index.reshape(8, 512))
    weights = jnp.concatenate(around_z(weight), 0)

    def rows_of(step):
        return lax.dynamic_slice(aggregate, (0, (y + step) % 4 * 256), (192, 256))

    rows = [rows_of(step) for step in range(4)]
    parts = [jnp.einsum("dr,dh->rh", block, weights, preferred_element_type=F32) for block in rows]
    preact = parts[0]
    for step in (1, 2, 3):
        preact = preact + along_y(parts[step].astype(BF), step).astype(F32)
    sigmoid_val = jax.nn.sigmoid(preact)
    hidden = (preact * sigmoid_val).astype(BF)
    pre_grad = (cotangent.astype(F32) * sigmoid_val * (1.0 + preact * (1.0 - sigmoid_val))).astype(BF)
    grad = jnp.dot(rows[0], pre_grad, preferred_element_type=F32)
    for step in (1, 2, 3):
        grad = grad + jnp.dot(rows[step], along_y(pre_grad, -step), preferred_element_type=F32)
    grad = grad.reshape(4, 48, 1024)
    weight_grad = grad[0]
    for step in (1, 2, 3):
        weight_grad = weight_grad + along_z(grad[step], step)
    for bit in (1, 2, 4):
        weight_grad = weight_grad + flip(weight_grad, bit)
    return hidden, weight_grad


def solution(mesh):
    placed = (
        P("feat", "batch"),
        P(None, "batch", None, None),
        P(None, "batch", None, None),
        P(),
        P("feat", None),
        P(("feat", "batch"), None),
    )
    return jax.shard_map(
        per_device,
        mesh=mesh,
        in_specs=placed,
        out_specs=(P(("feat", "batch"), None), P("feat", None)),
        check_vma=False,
    )
```

```python
import jax
import jax.numpy as jnp
from jax import lax
from jax.experimental import pallas as pl
from jax.experimental.pallas import tpu as pltpu
from jax.sharding import PartitionSpec as P

BF = jnp.bfloat16
F32 = jnp.float32
NT = (((1,), (1,)), ((), ()))


def edge_codes(slots, used):
    slot_row = lax.broadcasted_iota(jnp.int32, slots.shape, 0) & 15
    lane = lax.broadcasted_iota(jnp.int32, slots.shape, 1)
    height = slots.shape[0]
    value = jnp.where(slot_row < used, slots, -1)
    for bit in range(4):
        rows, lanes = 1 << bit, 8 << bit
        row_bit = (slot_row >> bit) & 1
        lane_bit = (lane >> (bit + 3)) & 1
        later = pltpu.roll(pltpu.roll(value, height - rows, 0), lanes, 1)
        earlier = pltpu.roll(pltpu.roll(value, rows, 0), 128 - lanes, 1)
        value = jnp.where(row_bit < lane_bit, later, jnp.where(row_bit > lane_bit, earlier, value))
    return (value >> 7) * 8 + (lane & 7), value & 127


def onehot(code):
    rows = lax.broadcasted_iota(jnp.int32, (128, 128), 0).astype(BF)
    match = jnp.broadcast_to(code.astype(BF), (128, 128)) == rows
    return jnp.where(match, BF(1), BF(0))


def build(adjacency, pairs_at, block, tile_codes, node_codes):
    blank = jnp.zeros((128, 128), BF)
    for pair in range(8):
        row = block * 16 + 2 * pair
        tile_a, tile_b = onehot(tile_codes[pl.ds(row, 1)]), onehot(tile_codes[pl.ds(row + 1, 1)])
        node_a, node_b = onehot(node_codes[pl.ds(row, 1)]), onehot(node_codes[pl.ds(row + 1, 1)])
        both = lax.dot_general(
            jnp.concatenate([tile_a, tile_b], 1),
            jnp.concatenate([jnp.concatenate([node_a, blank], 1), jnp.concatenate([blank, node_b], 1)], 0),
            NT,
            preferred_element_type=F32,
        )
        rows = jnp.concatenate([both[:, :128].reshape(16, 8, 128), both[:, 128:].reshape(16, 8, 128)], 1).astype(BF)
        for tile in range(16):
            adjacency[pairs_at, tile // 2, pair * 16:pair * 16 + 16, tile % 2 * 128:tile % 2 * 128 + 128] = rows[tile]


def remote(src, dst, sems, at, target):
    return pltpu.make_async_remote_copy(
        src_ref=src, dst_ref=dst, send_sem=sems.at[0, at], recv_sem=sems.at[1, at],
        device_id=target, device_id_type=pl.DeviceIdType.MESH,
    )


def layer_kernel(
    features, slots, counts, tiles, weight, cotangent, hidden, weight_grad,
    raw, near, far, slot_rows, used, tile_codes, node_codes, adjacency,
    core_near_out, core_near_in, core_far_out, core_far_in,
    x_near_out, x_near_in, x_far_out, x_far_in, own_near, own_far,
    weights, aggregate, rows, rows_t, cot, grad_out, grad_in, grad_y_out, grad_y_in, grad_own,
    grad_z_out, grad_z_in, grad_x_out, grad_x_in, pieces,
    load_sems, z_sems, w_sems, core_sems, x_sems, y_sems, grad_core_sems, grad_y_sems, grad_z_sems, grad_x_sems, piece_sems,
):
    feat, batch = lax.axis_index("feat"), lax.axis_index("batch")
    z, y, x, core = feat // 4, feat % 4, batch // 2, batch % 2
    piece = core * 4 + x

    def z_at(step):
        return (lax.rem(z + step, 4) * 4 + y, batch)

    def y_at(step):
        return (z * 4 + lax.rem(y + step, 4), batch)

    def x_at(step, side=0):
        return (feat, lax.rem(x + step, 4) * 2 + lax.rem(core + side, 2))

    partner = x_at(0, 1)
    others = [x_at(step, side) for step in range(4) for side in range(2)][1:]
    barrier = pltpu.get_barrier_semaphore()
    greeted = [z_at(1), z_at(2), z_at(3), y_at(1), y_at(2), y_at(3)] + others
    for device in greeted:
        pl.semaphore_signal(barrier, inc=1, device_id=device, device_id_type=pl.DeviceIdType.MESH)
    own_columns = pl.ds(pl.multiple_of(z * 1024, 1024), 1024)
    piece_columns = pl.ds(pl.multiple_of(piece * 128, 128), 128)
    loads = [
        pltpu.make_async_copy(features, raw, load_sems.at[0]),
        pltpu.make_async_copy(weight.at[:, piece_columns], weights.at[piece, pl.ds(0, 48)], load_sems.at[1]),
        pltpu.make_async_copy(slots.at[:, 0, :, own_columns], slot_rows, load_sems.at[2]),
        pltpu.make_async_copy(counts.at[:, :, own_columns], used, load_sems.at[3]),
        pltpu.make_async_copy(cotangent, cot, load_sems.at[4]),
    ]
    for load in loads:
        load.start()
    loads[0].wait()
    for tile in range(128):
        near[tile, 0:48, :] = raw[:, tile * 128:tile * 128 + 128]
    loads[1].wait()
    pl.semaphore_wait(barrier, len(greeted))

    low, high = pl.ds(0, 64), pl.ds(64, 64)

    def shard(at, part):
        return near.at[part, pl.ds(48 * at, 48), :]

    ring = [
        remote(shard(0, low), shard(2, low), z_sems, 0, z_at(1)),
        remote(shard(0, high), shard(1, high), z_sems, 1, z_at(3)),
        remote(shard(0, high), shard(2, high), z_sems, 2, z_at(1)),
        remote(shard(0, low), shard(1, low), z_sems, 3, z_at(3)),
        remote(shard(2, low), far.at[low], z_sems, 4, z_at(1)),
        remote(shard(1, high), far.at[high], z_sems, 5, z_at(3)),
    ]

    mine = weights.at[piece]
    w_first = mine.at[pl.ds(0, 48)]
    w_z = [
        remote(w_first, mine.at[pl.ds(48 * {1: 2, 2: 3, 3: 1}[step], 48)], w_sems, step - 1, z_at(step))
        for step in (1, 2, 3)
    ]
    w_y = [
        remote(mine.at[pl.ds(0, 192)], mine.at[pl.ds(192 * (4 - step), 192)], w_sems, 2 + step, y_at(step))
        for step in (1, 2, 3)
    ]
    w_all = [
        remote(mine, mine, w_sems, 6 + at, device) for at, device in enumerate(others)
    ]
    for copy in w_z:
        copy.start()
    ring[0].start()
    ring[1].start()
    loads[2].wait()
    loads[3].wait()

    def group_at(step):
        return lax.rem(x + 3 - step % 4, 4) * 2 + lax.rem(core + 1 - step // 4, 2)

    def build_group(step, unused):
        group = group_at(step)
        group_used = used[group, pl.ds(batch, 1), :]
        tile_code, node_code = edge_codes(
            jnp.concatenate([slot_rows[group, :, b * 128:b * 128 + 128] for b in range(8)], 0),
            jnp.concatenate([jnp.broadcast_to(group_used[:, b * 128:b * 128 + 128], (16, 128)) for b in range(8)], 0),
        )
        tile_codes[...] = tile_code
        node_codes[...] = node_code

        def some(turn, unused):
            for at in range(4):
                build(adjacency, step * 8 + turn * 4 + at, turn * 4 + at, tile_codes, node_codes)
            return 0

        return lax.fori_loop(0, 2, some, 0)

    lax.fori_loop(0, 2, build_group, 0)
    for copy in w_z:
        copy.wait_recv()
    for copy in w_y:
        copy.start()
    lax.fori_loop(2, 4, build_group, 0)
    ring[2].start()
    ring[3].start()
    for copy in w_y:
        copy.wait_recv()
    for copy in w_all:
        copy.start()
    lax.fori_loop(4, 8, build_group, 0)
    ring[0].wait_recv()
    ring[1].wait_recv()
    ring[4].start()
    ring[5].start()
    ring[2].wait_recv()
    ring[3].wait_recv()

    def products(feats, step, put):
        group = group_at(step)

        def one(block):
            total = jnp.zeros((feats.shape[1], 128), F32)
            for pair in range(8):
                entry = (z * 8 + block) * 16 + pair * 2
                halves = [feats[tiles[group, entry + half]] for half in range(2)]
                total += lax.dot_general(
                    jnp.concatenate(halves, 1), adjacency[step * 8 + block, pair], NT, preferred_element_type=F32
                )
            put(pl.ds(pl.multiple_of(block * 128, 128), 128), total)

        def some(turn, unused):
            for at in range(4):
                one(turn * 4 + at)
            return 0

        lax.fori_loop(0, 2, some, 0)

    def exchange(feats, core_out, core_in, x_out, x_in, own, core_base, x_base):
        def core_copy(at):
            return remote(core_out.at[at], core_in.at[at], core_sems, core_base + at, partner)

        def x_copy(at):
            return remote(x_out.at[at], x_in.at[at], x_sems, x_base + at, x_at(3 - at))

        def for_partner(step, unused):
            def put(columns, total):
                core_out[step, :, columns] = total

            products(feats, step, put)
            core_copy(step).start()
            return 0

        def for_x(at, unused):
            core_copy(at).wait_recv()

            def put(columns, total):
                x_out[at, :, columns] = (total + core_in[at, :, columns]).astype(BF)

            products(feats, at + 4, put)
            x_copy(at).start()
            return 0

        def put_own(columns, total):
            own[:, columns] = total + core_in[3, :, columns]

        lax.fori_loop(0, 4, for_partner, 0)
        lax.fori_loop(0, 3, for_x, 0)
        core_copy(3).wait_recv()
        products(feats, 7, put_own)
        return [core_copy(at) for at in range(4)], [x_copy(at) for at in range(3)]

    totals = jnp.sum(used[batch], axis=0, keepdims=True).astype(F32)

    def average(x_copies, own, x_in, first):
        for copy in x_copies:
            copy.wait_recv()
        height = own.shape[0]
        for chunk in range(4):
            columns = slice(chunk * 256, chunk * 256 + 256)
            summed = own[:, columns]
            for at in range(3):
                summed = summed + x_in[at, :, columns].astype(F32)
            aggregate[chunk, first:first + height, :] = (summed / totals[:, columns]).astype(BF)

    near_core, near_x = exchange(near, core_near_out, core_near_in, x_near_out, x_near_in, own_near, 0, 0)
    ring[4].wait_recv()
    ring[5].wait_recv()
    far_core, far_x = exchange(far, core_far_out, core_far_in, x_far_out, x_far_in, own_far, 4, 3)
    average(near_x, own_near, x_near_in, 0)
    average(far_x, own_far, x_far_in, 144)

    y_copies = [
        remote(aggregate.at[lax.rem(y + step, 4)], rows.at[4 - step], y_sems, step - 1, y_at(step)) for step in (1, 2, 3)
    ]
    for copy in y_copies:
        copy.start()
    rows[0] = aggregate[y]
    for copy in w_all:
        copy.wait_recv()
    loads[4].wait()
    for copy in y_copies:
        copy.wait_recv()
    rows_t[...] = rows[...].reshape(768, 256).T

    def layer(tile):
        columns = pl.ds(pl.multiple_of(tile * 256, 256), 256)
        preact = jnp.dot(
            rows_t[...], jnp.concatenate([weights[tile * 2], weights[tile * 2 + 1]], 1), preferred_element_type=F32
        )
        sigmoid_val = jax.nn.sigmoid(preact)
        hidden[:, columns] = (preact * sigmoid_val).astype(BF)
        pre_grad = cot[:, columns].astype(F32) * sigmoid_val * (1.0 + preact * (1.0 - sigmoid_val))
        return jnp.dot(rows[...].reshape(768, 256), pre_grad.astype(BF), preferred_element_type=F32)

    grad_core = [remote(grad_out.at[at], grad_in.at[at], grad_core_sems, at, partner) for at in range(2)]
    for at in range(2):
        grad_out[at] = layer((1 - core) * 2 + at)
        grad_core[at].start()
    grad_y = []
    for at in range(2):
        grad = layer(core * 2 + at)
        grad_core[at].wait_recv()
        grad = grad + grad_in[at]
        grad_own[at] = grad[0:192]
        for step in (1, 2, 3):
            slot = at * 3 + step - 1
            grad_y_out[slot] = grad[step * 192:step * 192 + 192].astype(BF)
            grad_y.append(remote(grad_y_out.at[slot], grad_y_in.at[slot], grad_y_sems, slot, y_at(step)))
            grad_y[slot].start()
    grad_z = []
    for at in range(2):
        grad = grad_own[at]
        for step in (1, 2, 3):
            grad_y[at * 3 + step - 1].wait_recv()
            grad = grad + grad_y_in[at * 3 + step - 1].astype(F32)
        grad_own[at] = grad
        for shard_at, step in ((1, 1), (2, 3), (3, 2)):
            slot = at * 3 + shard_at - 1
            grad_z_out[slot] = grad[shard_at * 48:shard_at * 48 + 48].astype(BF)
            grad_z.append(remote(grad_z_out.at[slot], grad_z_in.at[slot], grad_z_sems, slot, z_at(step)))
            grad_z[slot].start()
    for at in range(2):
        grad = grad_own[at, 0:48]
        for slot in range(at * 3, at * 3 + 3):
            grad_z[slot].wait_recv()
            grad = grad + grad_z_in[slot].astype(F32)
        grad_x_out[at * 2] = grad[:, :128]
        grad_x_out[at * 2 + 1] = grad[:, 128:]
    grad_x = [
        remote(grad_x_out.at[lax.rem(x + step, 4)], grad_x_in.at[step - 1], grad_x_sems, step - 1, x_at(step))
        for step in (1, 2, 3)
    ]
    for copy in grad_x:
        copy.start()
    grad = grad_x_out[x]
    for step in range(3):
        grad_x[step].wait_recv()
        grad = grad + grad_x_in[step]
    pieces[piece] = grad
    spread = [remote(pieces.at[piece], pieces.at[piece], piece_sems, at, device) for at, device in enumerate(others)]
    for copy in spread:
        copy.start()
    for copy in spread:
        copy.wait_recv()
    for at in range(8):
        weight_grad[:, at * 128:at * 128 + 128] = pieces[at]
    for copy in ring + w_z + w_y + w_all + near_core + near_x + far_core + far_x + y_copies + grad_core + grad_y + grad_z + grad_x + spread:
        copy.wait_send()


def per_device(features, sampled_slots, block_index, counts, weight, cotangent):
    hbm = pl.BlockSpec(memory_space=pl.ANY)
    vmem = pl.BlockSpec(memory_space=pltpu.VMEM)
    dma = pltpu.SemaphoreType.DMA
    return pl.pallas_call(
        layer_kernel,
        in_specs=[hbm, hbm, hbm, pl.BlockSpec(memory_space=pltpu.SMEM), hbm, hbm],
        out_specs=(vmem, vmem),
        scratch_shapes=[
            pltpu.VMEM((48, 16384), BF),
            pltpu.VMEM((128, 144, 128), BF),
            pltpu.VMEM((128, 48, 128), BF),
            pltpu.VMEM((8, 16, 1024), jnp.int32),
            pltpu.VMEM((8, 8, 1024), jnp.int32),
            pltpu.VMEM((128, 128), jnp.int32),
            pltpu.VMEM((128, 128), jnp.int32),
            pltpu.VMEM((64, 8, 128, 256), BF),
            pltpu.VMEM((4, 144, 1024), F32),
            pltpu.VMEM((4, 144, 1024), F32),
            pltpu.VMEM((4, 48, 1024), F32),
            pltpu.VMEM((4, 48, 1024), F32),
            pltpu.VMEM((3, 144, 1024), BF),
            pltpu.VMEM((3, 144, 1024), BF),
            pltpu.VMEM((3, 48, 1024), BF),
            pltpu.VMEM((3, 48, 1024), BF),
            pltpu.VMEM((144, 1024), F32),
            pltpu.VMEM((48, 1024), F32),
            pltpu.VMEM((8, 768, 128), BF),
            pltpu.VMEM((4, 192, 256), BF),
            pltpu.VMEM((4, 192, 256), BF),
            pltpu.VMEM((256, 768), BF),
            pltpu.VMEM((256, 1024), BF),
            pltpu.VMEM((2, 768, 256), F32),
            pltpu.VMEM((2, 768, 256), F32),
            pltpu.VMEM((6, 192, 256), BF),
            pltpu.VMEM((6, 192, 256), BF),
            pltpu.VMEM((2, 192, 256), F32),
            pltpu.VMEM((6, 48, 256), BF),
            pltpu.VMEM((6, 48, 256), BF),
            pltpu.VMEM((4, 48, 128), F32),
            pltpu.VMEM((3, 48, 128), F32),
            pltpu.VMEM((8, 48, 128), F32),
            dma((5,)), dma((2, 6)), dma((2, 13)), dma((2, 8)), dma((2, 6)), dma((2, 3)),
            dma((2, 2)), dma((2, 6)), dma((2, 6)), dma((2, 3)), dma((2, 7)),
        ],
        out_shape=(
            jax.ShapeDtypeStruct((256, 1024), BF),
            jax.ShapeDtypeStruct((48, 1024), F32),
        ),
        compiler_params=pltpu.CompilerParams(vmem_limit_bytes=63 << 20, collective_id=0, has_side_effects=True),
    )(features, sampled_slots, counts, block_index.reshape(8, 512), weight, cotangent)


def solution(mesh):
    placed = (
        P("feat", "batch"),
        P(None, "batch", None, None),
        P(None, "batch", None, None),
        P(),
        P("feat", None),
        P(("feat", "batch"), None),
    )
    return jax.shard_map(
        per_device,
        mesh=mesh,
        in_specs=placed,
        out_specs=(P(("feat", "batch"), None), P("feat", None)),
        check_vma=False,
    )
```

```python
import jax
import jax.numpy as jnp
from jax import lax
from jax.experimental import pallas as pl
from jax.experimental.pallas import tpu as pltpu
from jax.sharding import PartitionSpec as P

BF = jnp.bfloat16
F32 = jnp.float32
NT = (((1,), (1,)), ((), ()))


def edge_codes(slots, used):
    slot_row = lax.broadcasted_iota(jnp.int32, slots.shape, 0) & 15
    lane = lax.broadcasted_iota(jnp.int32, slots.shape, 1)
    height = slots.shape[0]
    value = jnp.where(slot_row < used, slots, -1)
    for bit in range(4):
        rows, lanes = 1 << bit, 8 << bit
        row_bit = (slot_row >> bit) & 1
        lane_bit = (lane >> (bit + 3)) & 1
        later = pltpu.roll(pltpu.roll(value, height - rows, 0), lanes, 1)
        earlier = pltpu.roll(pltpu.roll(value, rows, 0), 128 - lanes, 1)
        value = jnp.where(row_bit < lane_bit, later, jnp.where(row_bit > lane_bit, earlier, value))
    return (value >> 7) * 8 + (lane & 7), value & 127


def onehot(code):
    rows = lax.broadcasted_iota(jnp.int32, (128, 128), 0).astype(BF)
    match = jnp.broadcast_to(code.astype(BF), (128, 128)) == rows
    return jnp.where(match, BF(1), BF(0))


def build(adjacency, pairs_at, block, tile_codes, node_codes):
    blank = jnp.zeros((128, 128), BF)

    def diagonal(first, second):
        return jnp.concatenate([jnp.concatenate([first, blank], 1), jnp.concatenate([blank, second], 1)], 0)

    for pair in range(8):
        row = block * 16 + 2 * pair
        tile_a, tile_b = onehot(tile_codes[pl.ds(row, 1)]), onehot(tile_codes[pl.ds(row + 1, 1)])
        node_a, node_b = onehot(node_codes[pl.ds(row, 1)]), onehot(node_codes[pl.ds(row + 1, 1)])
        if pair % 2 == 0:
            left, right = jnp.concatenate([tile_a, tile_b], 1), diagonal(node_a, node_b)
        else:
            left, right = diagonal(tile_a, tile_b), jnp.concatenate([node_a, node_b], 1)
        both = lax.dot_general(left, right, NT, preferred_element_type=F32)
        both_a, both_b = (both[:, :128], both[:, 128:]) if pair % 2 == 0 else (both[:128], both[128:])
        rows = jnp.concatenate([both_a.reshape(16, 8, 128), both_b.reshape(16, 8, 128)], 1).astype(BF)
        for tile in range(16):
            adjacency[pairs_at, tile // 2, pair * 16:pair * 16 + 16, tile % 2 * 128:tile % 2 * 128 + 128] = rows[tile]


def remote(src, dst, sems, at, target):
    return pltpu.make_async_remote_copy(
        src_ref=src, dst_ref=dst, send_sem=sems.at[0, at], recv_sem=sems.at[1, at],
        device_id=target, device_id_type=pl.DeviceIdType.MESH,
    )


TURN = (0, 1, 3, 2)


def layer_kernel(
    features, slots, counts, tiles, weight, cotangent, hidden, weight_grad,
    raw, feats, slot_rows, used, own_used, tile_codes, node_codes, adjacency,
    sums_out, sums_in, x_out, x_in, weights, rows, rows_t, cot,
    grad_out, grad_in, grad_y_out, grad_y_in, grad_own, grad_z_out, grad_z_in, grad_x_out, grad_x_in, pieces,
    load_sems, ring_sems, w_sems, sum_sems, x_sems, grad_core_sems, grad_y_sems, grad_z_sems, grad_x_sems, piece_sems,
):
    feat, batch = lax.axis_index("feat"), lax.axis_index("batch")
    z, y, x, core = feat // 4, feat % 4, batch // 2, batch % 2
    piece = core * 4 + x
    ring_at_me, cross_at_me = z + core * (y - z), y + core * (z - y)

    def feat_at(ring_place, cross_place):
        return ring_place * (4 - 3 * core) + cross_place * (1 + 3 * core)

    def batch_at(step, side):
        return lax.rem(x + step, 4) * 2 + lax.rem(core + side, 2)

    def ring_dev(step, side=0):
        return (feat_at(lax.rem(ring_at_me + step, 4), cross_at_me), batch_at(0, side))

    def cross_dev(step, side=0):
        return (feat_at(ring_at_me, lax.rem(cross_at_me + step, 4)), batch_at(0, side))

    def x_at(step, side=0):
        return (feat, batch_at(step, side))

    partner = x_at(0, 1)
    others = [x_at(step, side) for step in range(4) for side in range(2)][1:]
    barrier = pltpu.get_barrier_semaphore()
    greeted = [dev(step, side) for dev in (ring_dev, cross_dev) for side in range(2) for step in (1, 2, 3)] + others
    for device in greeted:
        pl.semaphore_signal(barrier, inc=1, device_id=device, device_id_type=pl.DeviceIdType.MESH)

    def owned(owner):
        return pl.ds(pl.multiple_of(owner * 256, 256), 256)

    piece_columns = pl.ds(pl.multiple_of(piece * 128, 128), 128)
    loads = [
        pltpu.make_async_copy(features, raw, load_sems.at[0]),
        pltpu.make_async_copy(weight.at[:, piece_columns], weights.at[piece, pl.ds(0, 48)], load_sems.at[1]),
        pltpu.make_async_copy(cotangent, cot, load_sems.at[2]),
        pltpu.make_async_copy(counts.at[batch, :, owned(feat)], own_used, load_sems.at[3]),
    ]
    for at in range(4):
        source, target = owned(feat_at(ring_at_me, at)), pl.ds(at * 256, 256)
        loads.append(pltpu.make_async_copy(slots.at[:, 0, :, source], slot_rows.at[:, :, target], load_sems.at[4 + 2 * at]))
        loads.append(pltpu.make_async_copy(counts.at[:, :, source], used.at[:, :, target], load_sems.at[5 + 2 * at]))
    for load in loads:
        load.start()
    loads[0].wait()
    for tile in range(128):
        feats[tile, 0:48, :] = raw[:, tile * 128:tile * 128 + 128]
    loads[1].wait()
    pl.semaphore_wait(barrier, len(greeted))

    low, high = pl.ds(0, 64), pl.ds(64, 64)

    def shard(at, part):
        return feats.at[part, pl.ds(48 * at, 48), :]

    ring = [
        remote(shard(0, low), shard(2, low), ring_sems, 0, ring_dev(1)),
        remote(shard(0, high), shard(1, high), ring_sems, 1, ring_dev(3)),
        remote(shard(0, high), shard(2, high), ring_sems, 2, ring_dev(1)),
        remote(shard(0, low), shard(1, low), ring_sems, 3, ring_dev(3)),
        remote(shard(2, low), shard(3, low), ring_sems, 4, ring_dev(1)),
        remote(shard(1, high), shard(3, high), ring_sems, 5, ring_dev(3)),
    ]

    mine = weights.at[piece]
    w_first = mine.at[pl.ds(0, 48)]
    w_z = [
        remote(w_first, mine.at[pl.ds(48 * {1: 2, 2: 3, 3: 1}[step], 48)], w_sems, step - 1, ring_dev(step))
        for step in (1, 2, 3)
    ]
    w_y = [
        remote(mine.at[pl.ds(0, 192)], mine.at[pl.ds(192 * (4 - step), 192)], w_sems, 2 + step, cross_dev(step))
        for step in (1, 2, 3)
    ]
    w_all = [
        remote(mine, mine, w_sems, 6 + at, device) for at, device in enumerate(others)
    ]
    for copy in w_z:
        copy.start()
    ring[0].start()
    ring[1].start()
    for load in loads[4:]:
        load.wait()

    def group_at(step):
        turn = step // 2
        away = turn + 2 - (turn // 2) * (2 * turn - 1)
        return batch_at(away, 1 - step % 2)

    def build_group(step, unused):
        group = group_at(step)
        group_used = used[group, pl.ds(batch, 1), :]
        tile_code, node_code = edge_codes(
            jnp.concatenate([slot_rows[group, :, b * 128:b * 128 + 128] for b in range(8)], 0),
            jnp.concatenate([jnp.broadcast_to(group_used[:, b * 128:b * 128 + 128], (16, 128)) for b in range(8)], 0),
        )
        tile_codes[...] = tile_code
        node_codes[...] = node_code

        def some(turn, unused):
            for at in range(4):
                build(adjacency, step * 8 + turn * 4 + at, turn * 4 + at, tile_codes, node_codes)
            return 0

        return lax.fori_loop(0, 2, some, 0)

    lax.fori_loop(0, 2, build_group, 0)
    ring[2].start()
    ring[3].start()
    for copy in w_z:
        copy.wait_recv()
    for copy in w_y:
        copy.start()
    lax.fori_loop(2, 5, build_group, 0)
    ring[0].wait_recv()
    ring[1].wait_recv()
    ring[4].start()
    ring[5].start()
    for copy in w_y:
        copy.wait_recv()
    for copy in w_all:
        copy.start()
    lax.fori_loop(5, 8, build_group, 0)
    for at in (2, 3, 4, 5):
        ring[at].wait_recv()

    def products(step):
        group = group_at(step)

        def some(turn, unused):
            for at in range(4):
                owner = turn * 2 + at // 2
                block = feat_at(ring_at_me, owner) * 2 + at % 2
                total = jnp.zeros((192, 128), F32)
                for pair in range(8):
                    halves = [feats[tiles[group, block * 16 + pair * 2 + half]] for half in range(2)]
                    total += lax.dot_general(
                        jnp.concatenate(halves, 1),
                        adjacency[step * 8 + turn * 4 + at, pair],
                        NT,
                        preferred_element_type=F32,
                    )
                sums_out[step * 4 + owner, :, at % 2 * 128:at % 2 * 128 + 128] = total.astype(BF)
            return 0

        lax.fori_loop(0, 2, some, 0)

    def sum_copies(turn, side):
        copies = []
        for step in range(1 - side, 4):
            copies.append(
                remote(
                    sums_out.at[(turn * 2 + 1 - side) * 4 + lax.rem(cross_at_me + step, 4)],
                    sums_in.at[turn * 8 + side * 4 + (4 - step) % 4],
                    sum_sems, turn * 7 + side * 3 + step - 1 + side, cross_dev(step, side),
                )
            )
        return copies

    def owner_sum(turn, across):
        first = sums_out[(turn * 2 + 1) * 4 + cross_at_me] if across == 0 else sums_in[turn * 8 + across]
        second = [
            sums_in[turn * 8 + 4 + TURN[slot], TURN[across] * 48:TURN[across] * 48 + 48, :] for slot in range(4)
        ]
        return first.astype(F32) + jnp.concatenate(second, 0).astype(F32)

    x_steps = (2, 3, 1)
    x_copies = [remote(x_out.at[turn], x_in.at[turn], x_sems, turn, x_at(x_steps[turn])) for turn in range(3)]
    all_sums = []

    def finish(turn):
        for copy in all_sums[turn]:
            copy.wait_recv()
        if turn < 3:
            for across in range(4):
                x_out[turn, across * 192:across * 192 + 192, :] = owner_sum(turn, across).astype(BF)
            x_copies[turn].start()

    for turn in range(4):
        copies = []
        for side in (1, 0):
            products(turn * 2 + 1 - side)
            new = sum_copies(turn, side)
            for copy in new:
                copy.start()
            copies += new
            if side == 1 and turn > 0:
                finish(turn - 1)
        all_sums.append(copies)
    loads[2].wait()
    loads[3].wait()
    for copy in w_all:
        copy.wait_recv()
    totals = jnp.sum(own_used[...], axis=0, keepdims=True).astype(F32)
    finish(3)
    for copy in x_copies:
        copy.wait_recv()
    for across in range(4):
        part = slice(across * 192, across * 192 + 192)
        summed = owner_sum(3, across)
        for turn in range(3):
            summed = summed + x_in[turn, part, :].astype(F32)
        rows[part, :] = (summed / totals).astype(BF)
    rows_t[...] = rows[...].T

    def swapped(part):
        return jnp.concatenate(
            [part[TURN[slot] * 192 + TURN[across] * 48:TURN[slot] * 192 + TURN[across] * 48 + 48]
             for across in range(4) for slot in range(4)],
            0,
        )

    def layer(tile, partners):
        columns = pl.ds(pl.multiple_of(tile * 256, 256), 256)
        part = jnp.concatenate([weights[tile * 2], weights[tile * 2 + 1]], 1)
        preact = jnp.dot(rows_t[...], swapped(part) if partners else part, preferred_element_type=F32)
        sigmoid_val = jax.nn.sigmoid(preact)
        hidden[:, columns] = (preact * sigmoid_val).astype(BF)
        pre_grad = cot[:, columns].astype(F32) * sigmoid_val * (1.0 + preact * (1.0 - sigmoid_val))
        return jnp.dot(rows[...], pre_grad.astype(BF), preferred_element_type=F32)

    grad_core = [remote(grad_out.at[at], grad_in.at[at], grad_core_sems, at, partner) for at in range(2)]
    for at in range(2):
        grad_out[at] = layer((1 - core) * 2 + at, True)
        grad_core[at].start()
    grad_y = []
    for at in range(2):
        grad = layer(core * 2 + at, False)
        grad_core[at].wait_recv()
        grad = grad + swapped(grad_in[at])
        grad_own[at] = grad[0:192]
        for step in (1, 2, 3):
            slot = at * 3 + step - 1
            grad_y_out[slot] = grad[step * 192:step * 192 + 192].astype(BF)
            grad_y.append(remote(grad_y_out.at[slot], grad_y_in.at[slot], grad_y_sems, slot, cross_dev(step)))
            grad_y[slot].start()
    grad_z = []
    for at in range(2):
        grad = grad_own[at]
        for step in (1, 2, 3):
            grad_y[at * 3 + step - 1].wait_recv()
            grad = grad + grad_y_in[at * 3 + step - 1].astype(F32)
        grad_own[at] = grad
        for shard_at, step in ((1, 1), (2, 3), (3, 2)):
            slot = at * 3 + shard_at - 1
            grad_z_out[slot] = grad[shard_at * 48:shard_at * 48 + 48].astype(BF)
            grad_z.append(remote(grad_z_out.at[slot], grad_z_in.at[slot], grad_z_sems, slot, ring_dev(step)))
            grad_z[slot].start()
    for at in range(2):
        grad = grad_own[at, 0:48]
        for slot in range(at * 3, at * 3 + 3):
            grad_z[slot].wait_recv()
            grad = grad + grad_z_in[slot].astype(F32)
        grad_x_out[at * 2] = grad[:, :128]
        grad_x_out[at * 2 + 1] = grad[:, 128:]
    grad_x = [
        remote(grad_x_out.at[lax.rem(x + step, 4)], grad_x_in.at[step - 1], grad_x_sems, step - 1, x_at(step))
        for step in (1, 2, 3)
    ]
    for copy in grad_x:
        copy.start()
    grad = grad_x_out[x]
    for step in range(3):
        grad_x[step].wait_recv()
        grad = grad + grad_x_in[step]
    pieces[piece] = grad
    spread = [remote(pieces.at[piece], pieces.at[piece], piece_sems, at, device) for at, device in enumerate(others)]
    for copy in spread:
        copy.start()
    for copy in spread:
        copy.wait_recv()
    for at in range(8):
        weight_grad[:, at * 128:at * 128 + 128] = pieces[at]
    for copy in ring + w_z + w_y + w_all + sum(all_sums, []) + x_copies + grad_core + grad_y + grad_z + grad_x + spread:
        copy.wait_send()


def per_device(features, sampled_slots, block_index, counts, weight, cotangent):
    hbm = pl.BlockSpec(memory_space=pl.ANY)
    vmem = pl.BlockSpec(memory_space=pltpu.VMEM)
    dma = pltpu.SemaphoreType.DMA
    return pl.pallas_call(
        layer_kernel,
        in_specs=[hbm, hbm, hbm, pl.BlockSpec(memory_space=pltpu.SMEM), hbm, hbm],
        out_specs=(vmem, vmem),
        scratch_shapes=[
            pltpu.VMEM((48, 16384), BF),
            pltpu.VMEM((128, 192, 128), BF),
            pltpu.VMEM((8, 16, 1024), jnp.int32),
            pltpu.VMEM((8, 8, 1024), jnp.int32),
            pltpu.VMEM((8, 256), jnp.int32),
            pltpu.VMEM((128, 128), jnp.int32),
            pltpu.VMEM((128, 128), jnp.int32),
            pltpu.VMEM((64, 8, 128, 256), BF),
            pltpu.VMEM((32, 192, 256), BF),
            pltpu.VMEM((32, 192, 256), BF),
            pltpu.VMEM((3, 768, 256), BF),
            pltpu.VMEM((3, 768, 256), BF),
            pltpu.VMEM((8, 768, 128), BF),
            pltpu.VMEM((768, 256), BF),
            pltpu.VMEM((256, 768), BF),
            pltpu.VMEM((256, 1024), BF),
            pltpu.VMEM((2, 768, 256), F32),
            pltpu.VMEM((2, 768, 256), F32),
            pltpu.VMEM((6, 192, 256), BF),
            pltpu.VMEM((6, 192, 256), BF),
            pltpu.VMEM((2, 192, 256), F32),
            pltpu.VMEM((6, 48, 256), BF),
            pltpu.VMEM((6, 48, 256), BF),
            pltpu.VMEM((4, 48, 128), F32),
            pltpu.VMEM((3, 48, 128), F32),
            pltpu.VMEM((8, 48, 128), F32),
            dma((12,)), dma((2, 6)), dma((2, 13)), dma((2, 28)), dma((2, 3)),
            dma((2, 2)), dma((2, 6)), dma((2, 6)), dma((2, 3)), dma((2, 7)),
        ],
        out_shape=(
            jax.ShapeDtypeStruct((256, 1024), BF),
            jax.ShapeDtypeStruct((48, 1024), F32),
        ),
        compiler_params=pltpu.CompilerParams(vmem_limit_bytes=63 << 20, collective_id=0, has_side_effects=True),
    )(features, sampled_slots, counts, block_index.reshape(8, 512), weight, cotangent)


def solution(mesh):
    placed = (
        P("feat", "batch"),
        P(None, "batch", None, None),
        P(None, "batch", None, None),
        P(),
        P("feat", None),
        P(("feat", "batch"), None),
    )
    return jax.shard_map(
        per_device,
        mesh=mesh,
        in_specs=placed,
        out_specs=(P(("feat", "batch"), None), P("feat", None)),
        check_vma=False,
    )
```

```python
import jax
import jax.numpy as jnp
from jax import lax
from jax.experimental import pallas as pl
from jax.experimental.pallas import tpu as pltpu
from jax.sharding import PartitionSpec as P

BF = jnp.bfloat16
F32 = jnp.float32
NT = (((1,), (1,)), ((), ()))


def edge_codes(slots, used):
    slot_row = lax.broadcasted_iota(jnp.int32, slots.shape, 0) & 15
    lane = lax.broadcasted_iota(jnp.int32, slots.shape, 1)
    height = slots.shape[0]
    value = jnp.where(slot_row < used, slots, -1)
    for bit in range(4):
        rows, lanes = 1 << bit, 8 << bit
        row_bit = (slot_row >> bit) & 1
        lane_bit = (lane >> (bit + 3)) & 1
        later = pltpu.roll(pltpu.roll(value, height - rows, 0), lanes, 1)
        earlier = pltpu.roll(pltpu.roll(value, rows, 0), 128 - lanes, 1)
        value = jnp.where(row_bit < lane_bit, later, jnp.where(row_bit > lane_bit, earlier, value))
    return (value >> 7) * 8 + (lane & 7), value & 127


def onehot(code):
    rows = lax.broadcasted_iota(jnp.int32, (128, 128), 0).astype(BF)
    match = jnp.broadcast_to(code.astype(BF), (128, 128)) == rows
    return jnp.where(match, BF(1), BF(0))


def build(adjacency, pairs_at, block, tile_codes, node_codes):
    blank = jnp.zeros((128, 128), BF)

    def diagonal(first, second):
        return jnp.concatenate([jnp.concatenate([first, blank], 1), jnp.concatenate([blank, second], 1)], 0)

    for pair in range(8):
        row = block * 16 + 2 * pair
        tile_a, tile_b = onehot(tile_codes[pl.ds(row, 1)]), onehot(tile_codes[pl.ds(row + 1, 1)])
        node_a, node_b = onehot(node_codes[pl.ds(row, 1)]), onehot(node_codes[pl.ds(row + 1, 1)])
        if pair % 2 == 0:
            left, right = jnp.concatenate([tile_a, tile_b], 1), diagonal(node_a, node_b)
        else:
            left, right = diagonal(tile_a, tile_b), jnp.concatenate([node_a, node_b], 1)
        both = lax.dot_general(left, right, NT, preferred_element_type=F32)
        both_a, both_b = (both[:, :128], both[:, 128:]) if pair % 2 == 0 else (both[:128], both[128:])
        rows = jnp.concatenate([both_a.reshape(16, 8, 128), both_b.reshape(16, 8, 128)], 1).astype(BF)
        for tile in range(16):
            adjacency[pairs_at, tile // 2, pair * 16:pair * 16 + 16, tile % 2 * 128:tile % 2 * 128 + 128] = rows[tile]


def remote(src, dst, sems, at, target):
    return pltpu.make_async_remote_copy(
        src_ref=src, dst_ref=dst, send_sem=sems.at[0, at], recv_sem=sems.at[1, at],
        device_id=target, device_id_type=pl.DeviceIdType.MESH,
    )


TURN = (0, 1, 3, 2)


def layer_kernel(
    features, slots, counts, block_index, weight, cotangent, hidden, weight_grad,
    tiles, raw, feats, slot_rows, used, own_used, tile_codes, node_codes, adjacency,
    sums_out, sums_in, x_out, x_in, relay_in, weights, rows, rows_t, cot,
    grad_out, grad_in, grad_y_out, grad_y_in, grad_own, grad_own_slice, grad_z_out, grad_z_in, pieces,
    load_sems, ring_sems, w_sems, sum_sems, x_sems, grad_core_sems, grad_y_sems, grad_z_sems, piece_sems,
):
    feat, batch = lax.axis_index("feat"), lax.axis_index("batch")
    z, y, x, core = feat // 4, feat % 4, batch // 2, batch % 2
    piece = core * 4 + x
    ring_at_me, cross_at_me = z + core * (y - z), y + core * (z - y)

    def feat_at(ring_place, cross_place):
        return ring_place * (4 - 3 * core) + cross_place * (1 + 3 * core)

    def batch_at(step, side):
        return lax.rem(x + step, 4) * 2 + lax.rem(core + side, 2)

    def ring_dev(step, side=0):
        return (feat_at(lax.rem(ring_at_me + step, 4), cross_at_me), batch_at(0, side))

    def cross_dev(step, side=0):
        return (feat_at(ring_at_me, lax.rem(cross_at_me + step, 4)), batch_at(0, side))

    def x_at(step, side=0):
        return (feat, batch_at(step, side))

    partner = x_at(0, 1)
    others = [x_at(step, side) for step in range(4) for side in range(2)][1:]
    barrier = pltpu.get_barrier_semaphore()
    greeted = [dev(step, side) for dev in (ring_dev, cross_dev) for side in range(2) for step in (1, 2, 3)] + others
    greeted += [
        (feat_at(lax.rem(ring_at_me + step, 4), cross_at_me), batch_at(x_step, 0)) for step in (1, 2, 3) for x_step in (1, 2, 3)
    ]
    for device in greeted:
        pl.semaphore_signal(barrier, inc=1, device_id=device, device_id_type=pl.DeviceIdType.MESH)

    def owned(owner):
        return pl.ds(pl.multiple_of(owner * 256, 256), 256)

    piece_columns = pl.ds(pl.multiple_of(piece * 128, 128), 128)
    loads = [
        pltpu.make_async_copy(features, raw, load_sems.at[0]),
        pltpu.make_async_copy(weight.at[:, piece_columns], weights.at[piece, pl.ds(0, 48)], load_sems.at[1]),
        pltpu.make_async_copy(cotangent, cot, load_sems.at[2]),
        pltpu.make_async_copy(counts.at[batch, :, owned(feat)], own_used, load_sems.at[3]),
        pltpu.make_async_copy(block_index.at[:, 0], tiles, load_sems.at[12]),
    ]
    for at in range(4):
        source, target = owned(feat_at(ring_at_me, at)), pl.ds(at * 256, 256)
        loads.append(pltpu.make_async_copy(slots.at[:, 0, :, source], slot_rows.at[:, :, target], load_sems.at[4 + 2 * at]))
        loads.append(pltpu.make_async_copy(counts.at[:, :, source], used.at[:, :, target], load_sems.at[5 + 2 * at]))
    for load in loads:
        load.start()
    loads[0].wait()
    for tile in range(128):
        feats[tile, 0:48, :] = raw[:, tile * 128:tile * 128 + 128]
    loads[1].wait()
    pl.semaphore_wait(barrier, len(greeted))

    low, high = pl.ds(0, 64), pl.ds(64, 64)

    def shard(at, part):
        return feats.at[part, pl.ds(48 * at, 48), :]

    ring = [
        remote(shard(0, low), shard(2, low), ring_sems, 0, ring_dev(1)),
        remote(shard(0, high), shard(1, high), ring_sems, 1, ring_dev(3)),
        remote(shard(0, high), shard(2, high), ring_sems, 2, ring_dev(1)),
        remote(shard(0, low), shard(1, low), ring_sems, 3, ring_dev(3)),
        remote(shard(2, low), shard(3, low), ring_sems, 4, ring_dev(1)),
        remote(shard(1, high), shard(3, high), ring_sems, 5, ring_dev(3)),
    ]

    mine = weights.at[piece]
    w_first = mine.at[pl.ds(0, 48)]
    w_z = [
        remote(w_first, mine.at[pl.ds(48 * {1: 2, 2: 3, 3: 1}[step], 48)], w_sems, step - 1, ring_dev(step))
        for step in (1, 2, 3)
    ]
    w_y = [
        remote(mine.at[pl.ds(0, 192)], mine.at[pl.ds(192 * (4 - step), 192)], w_sems, 2 + step, cross_dev(step))
        for step in (1, 2, 3)
    ]
    w_all = [
        remote(mine, mine, w_sems, 6 + at, device) for at, device in enumerate(others)
    ]
    for copy in w_z:
        copy.start()
    ring[0].start()
    ring[1].start()
    for load in loads[4:]:
        load.wait()

    def group_at(step):
        turn = step // 2
        away = turn + 2 - (turn // 2) * (2 * turn - 1)
        return batch_at(away, 1 - step % 2)

    def build_group(step, unused):
        group = group_at(step)
        group_used = used[group, pl.ds(batch, 1), :]
        tile_code, node_code = edge_codes(
            jnp.concatenate([slot_rows[group, :, b * 128:b * 128 + 128] for b in range(8)], 0),
            jnp.concatenate([jnp.broadcast_to(group_used[:, b * 128:b * 128 + 128], (16, 128)) for b in range(8)], 0),
        )
        tile_codes[...] = tile_code
        node_codes[...] = node_code

        def some(turn, unused):
            for at in range(4):
                build(adjacency, step * 8 + turn * 4 + at, turn * 4 + at, tile_codes, node_codes)
            return 0

        return lax.fori_loop(0, 2, some, 0)

    lax.fori_loop(0, 2, build_group, 0)
    ring[2].start()
    ring[3].start()
    for copy in w_z:
        copy.wait_recv()
    for copy in w_y:
        copy.start()
    lax.fori_loop(2, 5, build_group, 0)
    ring[0].wait_recv()
    ring[1].wait_recv()
    ring[4].start()
    ring[5].start()
    for copy in w_y:
        copy.wait_recv()
    for copy in w_all:
        copy.start()
    lax.fori_loop(5, 8, build_group, 0)
    for at in (2, 3, 4, 5):
        ring[at].wait_recv()

    def products(step):
        group = group_at(step)

        def some(turn, unused):
            for at in range(4):
                owner = turn * 2 + at // 2
                block = feat_at(ring_at_me, owner) * 2 + at % 2
                total = jnp.zeros((192, 128), F32)
                for pair in range(8):
                    halves = [feats[tiles[group, pair * 2 + half, block]] for half in range(2)]
                    total += lax.dot_general(
                        jnp.concatenate(halves, 1),
                        adjacency[step * 8 + turn * 4 + at, pair],
                        NT,
                        preferred_element_type=F32,
                    )
                sums_out[step * 4 + owner, :, at % 2 * 128:at % 2 * 128 + 128] = total.astype(BF)
            return 0

        lax.fori_loop(0, 2, some, 0)

    def sum_copies(turn, side):
        copies = []
        for step in range(1 - side, 4):
            copies.append(
                remote(
                    sums_out.at[(turn * 2 + 1 - side) * 4 + lax.rem(cross_at_me + step, 4)],
                    sums_in.at[turn * 8 + side * 4 + (4 - step) % 4],
                    sum_sems, turn * 7 + side * 3 + step - 1 + side, cross_dev(step, side),
                )
            )
        return copies

    def owner_sum(turn, across):
        first = sums_out[(turn * 2 + 1) * 4 + cross_at_me] if across == 0 else sums_in[turn * 8 + across]
        second = [
            sums_in[turn * 8 + 4 + TURN[slot], TURN[across] * 48:TURN[across] * 48 + 48, :] for slot in range(4)
        ]
        return first.astype(F32) + jnp.concatenate(second, 0).astype(F32)

    relays = [
        remote(x_out.at[0, pl.ds(384 * at, 384)], relay_in.at[at], x_sems, at, x_at(1 + 2 * at)) for at in range(2)
    ]
    x_copies = [remote(x_out.at[1 + at], x_in.at[at], x_sems, 2 + at, x_at(3 - 2 * at)) for at in range(2)]
    all_sums = []

    def finish(turn):
        for copy in all_sums[turn]:
            copy.wait_recv()
        if turn == 3:
            return
        if turn > 0:
            relays[2 - turn].wait_recv()
        for across in range(4):
            total = owner_sum(turn, across)
            if turn > 0 and across // 2 == 2 - turn:
                total = total + relay_in[across // 2, across % 2 * 192:across % 2 * 192 + 192, :].astype(F32)
            x_out[turn, across * 192:across * 192 + 192, :] = total.astype(BF)
        for copy in relays if turn == 0 else [x_copies[turn - 1]]:
            copy.start()

    for turn in range(4):
        copies = []
        for side in (1, 0):
            products(turn * 2 + 1 - side)
            new = sum_copies(turn, side)
            for copy in new:
                copy.start()
            copies += new
            if side == 1 and turn > 0:
                finish(turn - 1)
        all_sums.append(copies)
    loads[2].wait()
    loads[3].wait()
    for copy in w_all:
        copy.wait_recv()
    totals = jnp.sum(own_used[...], axis=0, keepdims=True).astype(F32)
    finish(3)
    for copy in x_copies:
        copy.wait_recv()
    for across in range(4):
        part = slice(across * 192, across * 192 + 192)
        summed = owner_sum(3, across)
        for turn in range(2):
            summed = summed + x_in[turn, part, :].astype(F32)
        rows[part, :] = (summed / totals).astype(BF)
    rows_t[...] = rows[...].T

    def swapped(part):
        return jnp.concatenate(
            [part[TURN[slot] * 192 + TURN[across] * 48:TURN[slot] * 192 + TURN[across] * 48 + 48]
             for across in range(4) for slot in range(4)],
            0,
        )

    def layer(tile, partners):
        columns = pl.ds(pl.multiple_of(tile * 256, 256), 256)
        part = jnp.concatenate([weights[tile * 2], weights[tile * 2 + 1]], 1)
        preact = jnp.dot(rows_t[...], swapped(part) if partners else part, preferred_element_type=F32)
        sigmoid_val = jax.nn.sigmoid(preact)
        hidden[:, columns] = (preact * sigmoid_val).astype(BF)
        pre_grad = cot[:, columns].astype(F32) * sigmoid_val * (1.0 + preact * (1.0 - sigmoid_val))
        return jnp.dot(rows[...], pre_grad.astype(BF), preferred_element_type=F32)

    grad_core = [remote(grad_out.at[at], grad_in.at[at], grad_core_sems, at, partner) for at in range(2)]
    for at in range(2):
        grad_out[at] = layer((1 - core) * 2 + at, True)
        grad_core[at].start()
    grad_y = []
    for at in range(2):
        grad = layer(core * 2 + at, False)
        grad_core[at].wait_recv()
        grad = grad + swapped(grad_in[at])
        grad_own[at] = grad[0:192]
        for step in (1, 2, 3):
            slot = at * 3 + step - 1
            grad_y_out[slot] = grad[step * 192:step * 192 + 192].astype(BF)
            grad_y.append(remote(grad_y_out.at[slot], grad_y_in.at[slot], grad_y_sems, slot, cross_dev(step)))
            grad_y[slot].start()
    for at in range(2):
        grad = grad_own[at]
        for step in (1, 2, 3):
            grad_y[at * 3 + step - 1].wait_recv()
            grad = grad + grad_y_in[at * 3 + step - 1].astype(F32)
        for half in range(2):
            columns = slice(half * 128, half * 128 + 128)
            grad_own_slice[at * 2 + half] = grad[0:48, columns]
            for slot in range(4):
                grad_z_out[(at * 2 + half) * 4 + slot] = grad[slot * 48:slot * 48 + 48, columns].astype(BF)
    grad_z = [
        remote(
            grad_z_out.at[lax.rem(x + step, 4) * 4 + slot], grad_z_in.at[step * 4 + slot - 1], grad_z_sems, step * 4 + slot - 1,
            (feat_at(lax.rem(ring_at_me + TURN[slot], 4), cross_at_me), batch_at(step, 0)),
        )
        for step in range(4) for slot in range(4) if step + slot > 0
    ]
    for copy in grad_z:
        copy.start()
    grad = grad_own_slice[x]
    for at in range(15):
        grad_z[at].wait_recv()
        grad = grad + grad_z_in[at].astype(F32)
    pieces[piece] = grad
    spread = [remote(pieces.at[piece], pieces.at[piece], piece_sems, at, device) for at, device in enumerate(others)]
    for copy in spread:
        copy.start()
    for copy in spread:
        copy.wait_recv()
    for at in range(8):
        weight_grad[:, at * 128:at * 128 + 128] = pieces[at]
    for copy in ring + w_z + w_y + w_all + sum(all_sums, []) + relays + x_copies + grad_core + grad_y + grad_z + spread:
        copy.wait_send()


def place_kernel(hidden, weight_grad, hidden_out, weight_grad_out, sems):
    copies = [
        pltpu.make_async_copy(hidden, hidden_out, sems.at[0]),
        pltpu.make_async_copy(weight_grad, weight_grad_out, sems.at[1]),
    ]
    for copy in copies:
        copy.start()
    for copy in copies:
        copy.wait()


def per_device(features, sampled_slots, block_index, counts, weight, cotangent):
    hbm = pl.BlockSpec(memory_space=pl.ANY)
    vmem = pl.BlockSpec(memory_space=pltpu.VMEM)
    dma = pltpu.SemaphoreType.DMA
    outs = pl.pallas_call(
        layer_kernel,
        in_specs=[hbm] * 6,
        out_specs=(vmem, vmem),
        scratch_shapes=[
            pltpu.SMEM((8, 16, 32), jnp.int32),
            pltpu.VMEM((48, 16384), BF),
            pltpu.VMEM((128, 192, 128), BF),
            pltpu.VMEM((8, 16, 1024), jnp.int32),
            pltpu.VMEM((8, 8, 1024), jnp.int32),
            pltpu.VMEM((8, 256), jnp.int32),
            pltpu.VMEM((128, 128), jnp.int32),
            pltpu.VMEM((128, 128), jnp.int32),
            pltpu.VMEM((64, 8, 128, 256), BF),
            pltpu.VMEM((32, 192, 256), BF),
            pltpu.VMEM((32, 192, 256), BF),
            pltpu.VMEM((3, 768, 256), BF),
            pltpu.VMEM((2, 768, 256), BF),
            pltpu.VMEM((2, 384, 256), BF),
            pltpu.VMEM((8, 768, 128), BF),
            pltpu.VMEM((768, 256), BF),
            pltpu.VMEM((256, 768), BF),
            pltpu.VMEM((256, 1024), BF),
            pltpu.VMEM((2, 768, 256), F32),
            pltpu.VMEM((2, 768, 256), F32),
            pltpu.VMEM((6, 192, 256), BF),
            pltpu.VMEM((6, 192, 256), BF),
            pltpu.VMEM((2, 192, 256), F32),
            pltpu.VMEM((4, 48, 128), F32),
            pltpu.VMEM((16, 48, 128), BF),
            pltpu.VMEM((15, 48, 128), BF),
            pltpu.VMEM((8, 48, 128), F32),
            dma((13,)), dma((2, 6)), dma((2, 13)), dma((2, 28)), dma((2, 4)),
            dma((2, 2)), dma((2, 6)), dma((2, 15)), dma((2, 7)),
        ],
        out_shape=(
            jax.ShapeDtypeStruct((256, 1024), BF),
            jax.ShapeDtypeStruct((48, 1024), F32),
        ),
        compiler_params=pltpu.CompilerParams(vmem_limit_bytes=63 << 20, collective_id=0, has_side_effects=True),
    )(features, sampled_slots, counts, jnp.swapaxes(block_index, 2, 3), weight, cotangent)
    return pl.pallas_call(
        place_kernel,
        in_specs=[hbm, hbm],
        out_specs=(hbm, hbm),
        scratch_shapes=[dma((2,))],
        out_shape=(
            jax.ShapeDtypeStruct((256, 1024), BF),
            jax.ShapeDtypeStruct((48, 1024), F32),
        ),
        compiler_params=pltpu.CompilerParams(vmem_limit_bytes=63 << 20),
    )(*outs)


def solution(mesh):
    placed = (
        P("feat", "batch"),
        P(None, "batch", None, None),
        P(None, "batch", None, None),
        P(),
        P("feat", None),
        P(("feat", "batch"), None),
    )
    return jax.shard_map(
        per_device,
        mesh=mesh,
        in_specs=placed,
        out_specs=(P(("feat", "batch"), None), P("feat", None)),
        check_vma=False,
    )
```

```python
import jax
import jax.numpy as jnp
from jax import lax
from jax.experimental import pallas as pl
from jax.experimental.pallas import tpu as pltpu
from jax.sharding import PartitionSpec as P

BF = jnp.bfloat16
F32 = jnp.float32
NT = (((1,), (1,)), ((), ()))


def edge_codes(slots, used):
    slot_row = lax.broadcasted_iota(jnp.int32, slots.shape, 0) & 15
    lane = lax.broadcasted_iota(jnp.int32, slots.shape, 1)
    height = slots.shape[0]
    value = jnp.where(slot_row < used, slots, -1)
    for bit in range(4):
        rows, lanes = 1 << bit, 8 << bit
        row_bit = (slot_row >> bit) & 1
        lane_bit = (lane >> (bit + 3)) & 1
        later = pltpu.roll(pltpu.roll(value, height - rows, 0), lanes, 1)
        earlier = pltpu.roll(pltpu.roll(value, rows, 0), 128 - lanes, 1)
        value = jnp.where(row_bit < lane_bit, later, jnp.where(row_bit > lane_bit, earlier, value))
    return (value >> 7) * 8 + (lane & 7), value & 127


def onehot(code):
    rows = lax.broadcasted_iota(jnp.int32, (128, 128), 0).astype(BF)
    match = jnp.broadcast_to(code.astype(BF), (128, 128)) == rows
    return jnp.where(match, BF(1), BF(0))


def build(adjacency, pairs_at, block, tile_codes, node_codes):
    blank = jnp.zeros((128, 128), BF)

    def diagonal(first, second):
        return jnp.concatenate([jnp.concatenate([first, blank], 1), jnp.concatenate([blank, second], 1)], 0)

    for pair in range(8):
        row = block * 16 + 2 * pair
        tile_a, tile_b = onehot(tile_codes[pl.ds(row, 1)]), onehot(tile_codes[pl.ds(row + 1, 1)])
        node_a, node_b = onehot(node_codes[pl.ds(row, 1)]), onehot(node_codes[pl.ds(row + 1, 1)])
        if pair % 2 == 0:
            left, right = jnp.concatenate([tile_a, tile_b], 1), diagonal(node_a, node_b)
        else:
            left, right = diagonal(tile_a, tile_b), jnp.concatenate([node_a, node_b], 1)
        both = lax.dot_general(left, right, NT, preferred_element_type=F32)
        both_a, both_b = (both[:, :128], both[:, 128:]) if pair % 2 == 0 else (both[:128], both[128:])
        rows = jnp.concatenate([both_a.reshape(16, 8, 128), both_b.reshape(16, 8, 128)], 1).astype(BF)
        for tile in range(16):
            adjacency[pairs_at, tile // 2, pair * 16:pair * 16 + 16, tile % 2 * 128:tile % 2 * 128 + 128] = rows[tile]


def remote(src, dst, sems, at, target):
    return pltpu.make_async_remote_copy(
        src_ref=src, dst_ref=dst, send_sem=sems.at[0, at], recv_sem=sems.at[1, at],
        device_id=target, device_id_type=pl.DeviceIdType.MESH,
    )


TURN = (0, 1, 3, 2)


def layer_kernel(
    features, slots, counts, block_index, weight, cotangent, hidden, weight_grad,
    tiles, raw, feats, slot_rows, used, own_used, tile_codes, node_codes, adjacency,
    sums_out, sums_in, x_out, x_in, relay_in, weights, rows, rows_t, cot,
    grad_out, grad_in, grad_y_out, grad_y_in, grad_own, grad_own_slice, grad_z_out, grad_z_in, pieces,
    load_sems, ring_sems, w_sems, sum_sems, x_sems, grad_core_sems, grad_y_sems, grad_z_sems, piece_sems,
):
    feat, batch = lax.axis_index("feat"), lax.axis_index("batch")
    z, y, x, core = feat // 4, feat % 4, batch // 2, batch % 2
    piece = core * 4 + x
    ring_at_me, cross_at_me = z + core * (y - z), y + core * (z - y)

    def feat_at(ring_place, cross_place):
        return ring_place * (4 - 3 * core) + cross_place * (1 + 3 * core)

    def batch_at(step, side):
        return lax.rem(x + step, 4) * 2 + lax.rem(core + side, 2)

    def ring_dev(step, side=0):
        return (feat_at(lax.rem(ring_at_me + step, 4), cross_at_me), batch_at(0, side))

    def cross_dev(step, side=0):
        return (feat_at(ring_at_me, lax.rem(cross_at_me + step, 4)), batch_at(0, side))

    def x_at(step, side=0):
        return (feat, batch_at(step, side))

    partner = x_at(0, 1)
    others = [x_at(step, side) for step in range(4) for side in range(2)][1:]
    barrier = pltpu.get_barrier_semaphore()
    greeted = [dev(step, side) for dev in (ring_dev, cross_dev) for side in range(2) for step in (1, 2, 3)] + others
    greeted += [
        (feat_at(lax.rem(ring_at_me + step, 4), cross_at_me), batch_at(x_step, 0)) for step in (1, 2, 3) for x_step in (1, 2, 3)
    ]
    for device in greeted:
        pl.semaphore_signal(barrier, inc=1, device_id=device, device_id_type=pl.DeviceIdType.MESH)

    def owned(owner):
        return pl.ds(pl.multiple_of(owner * 256, 256), 256)

    piece_columns = pl.ds(pl.multiple_of(piece * 128, 128), 128)
    loads = [
        pltpu.make_async_copy(features, raw, load_sems.at[0]),
        pltpu.make_async_copy(weight.at[:, piece_columns], weights.at[piece, pl.ds(0, 48)], load_sems.at[1]),
        pltpu.make_async_copy(cotangent, cot, load_sems.at[2]),
        pltpu.make_async_copy(counts.at[batch, :, owned(feat)], own_used, load_sems.at[3]),
        pltpu.make_async_copy(block_index.at[:, 0], tiles, load_sems.at[12]),
    ]
    for at in range(4):
        source, target = owned(feat_at(ring_at_me, at)), pl.ds(at * 256, 256)
        loads.append(pltpu.make_async_copy(slots.at[:, 0, :, source], slot_rows.at[:, :, target], load_sems.at[4 + 2 * at]))
        loads.append(pltpu.make_async_copy(counts.at[:, :, source], used.at[:, :, target], load_sems.at[5 + 2 * at]))
    for load in loads:
        load.start()
    loads[0].wait()
    for tile in range(128):
        feats[tile, 0:48, :] = raw[:, tile * 128:tile * 128 + 128]
    loads[1].wait()
    pl.semaphore_wait(barrier, len(greeted))

    low, high = pl.ds(0, 64), pl.ds(64, 64)

    def shard(at, part):
        return feats.at[part, pl.ds(48 * at, 48), :]

    ring = [
        remote(shard(0, low), shard(2, low), ring_sems, 0, ring_dev(1)),
        remote(shard(0, high), shard(1, high), ring_sems, 1, ring_dev(3)),
        remote(shard(0, high), shard(2, high), ring_sems, 2, ring_dev(1)),
        remote(shard(0, low), shard(1, low), ring_sems, 3, ring_dev(3)),
        remote(shard(2, low), shard(3, low), ring_sems, 4, ring_dev(1)),
        remote(shard(1, high), shard(3, high), ring_sems, 5, ring_dev(3)),
    ]

    mine = weights.at[piece]
    w_first = mine.at[pl.ds(0, 48)]
    w_z = [
        remote(w_first, mine.at[pl.ds(48 * {1: 2, 2: 3, 3: 1}[step], 48)], w_sems, step - 1, ring_dev(step))
        for step in (1, 2, 3)
    ]
    w_y = [
        remote(mine.at[pl.ds(0, 192)], mine.at[pl.ds(192 * (4 - step), 192)], w_sems, 2 + step, cross_dev(step))
        for step in (1, 2, 3)
    ]
    w_all = [
        remote(mine, mine, w_sems, 6 + at, device) for at, device in enumerate(others)
    ]
    for copy in w_z:
        copy.start()
    ring[0].start()
    ring[1].start()
    for load in loads[4:]:
        load.wait()

    def group_at(step):
        turn = step // 2
        away = turn + 2 - (turn // 2) * (2 * turn - 1)
        return batch_at(away, 1 - step % 2)

    def build_group(step, unused):
        group = group_at(step)
        group_used = used[group, pl.ds(batch, 1), :]
        tile_code, node_code = edge_codes(
            jnp.concatenate([slot_rows[group, :, b * 128:b * 128 + 128] for b in range(8)], 0),
            jnp.concatenate([jnp.broadcast_to(group_used[:, b * 128:b * 128 + 128], (16, 128)) for b in range(8)], 0),
        )
        tile_codes[...] = tile_code
        node_codes[...] = node_code

        def some(turn, unused):
            for at in range(4):
                build(adjacency, step * 8 + turn * 4 + at, turn * 4 + at, tile_codes, node_codes)
            return 0

        return lax.fori_loop(0, 2, some, 0)

    lax.fori_loop(0, 2, build_group, 0)
    ring[2].start()
    ring[3].start()
    for copy in w_z:
        copy.wait_recv()
    for copy in w_y:
        copy.start()
    lax.fori_loop(2, 5, build_group, 0)
    ring[0].wait_recv()
    ring[1].wait_recv()
    ring[4].start()
    ring[5].start()
    for copy in w_y:
        copy.wait_recv()
    for copy in w_all:
        copy.start()
    lax.fori_loop(5, 8, build_group, 0)
    for at in (2, 3, 4, 5):
        ring[at].wait_recv()

    def products(step):
        group = group_at(step)

        def some(turn, unused):
            for at in range(4):
                owner = turn * 2 + at // 2
                block = feat_at(ring_at_me, owner) * 2 + at % 2
                total = jnp.zeros((192, 128), F32)
                for pair in range(8):
                    halves = [feats[tiles[group, pair * 2 + half, block]] for half in range(2)]
                    total += lax.dot_general(
                        jnp.concatenate(halves, 1),
                        adjacency[step * 8 + turn * 4 + at, pair],
                        NT,
                        preferred_element_type=F32,
                    )
                sums_out[step * 4 + owner, :, at % 2 * 128:at % 2 * 128 + 128] = total.astype(BF)
            return 0

        lax.fori_loop(0, 2, some, 0)

    def sum_copies(turn, side):
        copies = []
        for step in range(1 - side, 4):
            copies.append(
                remote(
                    sums_out.at[(turn * 2 + 1 - side) * 4 + lax.rem(cross_at_me + step, 4)],
                    sums_in.at[turn * 8 + side * 4 + (4 - step) % 4],
                    sum_sems, turn * 7 + side * 3 + step - 1 + side, cross_dev(step, side),
                )
            )
        return copies

    def owner_sum(turn, across):
        first = sums_out[(turn * 2 + 1) * 4 + cross_at_me] if across == 0 else sums_in[turn * 8 + across]
        second = [
            sums_in[turn * 8 + 4 + TURN[slot], TURN[across] * 48:TURN[across] * 48 + 48, :] for slot in range(4)
        ]
        return first.astype(F32) + jnp.concatenate(second, 0).astype(F32)

    relays = [
        remote(x_out.at[0, pl.ds(384 * at, 384)], relay_in.at[at], x_sems, at, x_at(1 + 2 * at)) for at in range(2)
    ]
    x_copies = [remote(x_out.at[1 + at], x_in.at[at], x_sems, 2 + at, x_at(3 - 2 * at)) for at in range(2)]
    all_sums = []

    def finish(turn):
        for copy in all_sums[turn]:
            copy.wait_recv()
        if turn == 3:
            return
        if turn > 0:
            relays[2 - turn].wait_recv()
        for across in range(4):
            total = owner_sum(turn, across)
            if turn > 0 and across // 2 == 2 - turn:
                total = total + relay_in[across // 2, across % 2 * 192:across % 2 * 192 + 192, :].astype(F32)
            x_out[turn, across * 192:across * 192 + 192, :] = total.astype(BF)
        for copy in relays if turn == 0 else [x_copies[turn - 1]]:
            copy.start()

    for turn in range(4):
        copies = []
        for side in (1, 0):
            products(turn * 2 + 1 - side)
            new = sum_copies(turn, side)
            for copy in new:
                copy.start()
            copies += new
            if side == 1 and turn > 0:
                finish(turn - 1)
        all_sums.append(copies)
    loads[2].wait()
    loads[3].wait()
    for copy in w_all:
        copy.wait_recv()
    totals = jnp.sum(own_used[...], axis=0, keepdims=True).astype(F32)
    finish(3)
    for copy in x_copies:
        copy.wait_recv()
    for across in range(4):
        part = slice(across * 192, across * 192 + 192)
        summed = owner_sum(3, across)
        for turn in range(2):
            summed = summed + x_in[turn, part, :].astype(F32)
        rows[part, :] = (summed / totals).astype(BF)
    rows_t[...] = rows[...].T

    def swapped(part):
        return jnp.concatenate(
            [part[TURN[slot] * 192 + TURN[across] * 48:TURN[slot] * 192 + TURN[across] * 48 + 48]
             for across in range(4) for slot in range(4)],
            0,
        )

    def layer(tile, partners):
        columns = pl.ds(pl.multiple_of(tile * 256, 256), 256)
        part = jnp.concatenate([weights[tile * 2], weights[tile * 2 + 1]], 1)
        preact = jnp.dot(rows_t[...], swapped(part) if partners else part, preferred_element_type=F32)
        sigmoid_val = jax.nn.sigmoid(preact)
        hidden[:, columns] = (preact * sigmoid_val).astype(BF)
        pre_grad = cot[:, columns].astype(F32) * sigmoid_val * (1.0 + preact * (1.0 - sigmoid_val))
        return jnp.dot(rows[...], pre_grad.astype(BF), preferred_element_type=F32)

    grad_core = [remote(grad_out.at[at], grad_in.at[at], grad_core_sems, at, partner) for at in range(2)]
    for at in range(2):
        grad_out[at] = layer((1 - core) * 2 + at, True)
        grad_core[at].start()
    grad_y = []
    for at in range(2):
        grad = layer(core * 2 + at, False)
        grad_core[at].wait_recv()
        grad = grad + swapped(grad_in[at])
        grad_own[at] = grad[0:192]
        for step in (1, 2, 3):
            slot = at * 3 + step - 1
            grad_y_out[slot] = grad[step * 192:step * 192 + 192].astype(BF)
            grad_y.append(remote(grad_y_out.at[slot], grad_y_in.at[slot], grad_y_sems, slot, cross_dev(step)))
            grad_y[slot].start()
    for at in range(2):
        grad = grad_own[at]
        for step in (1, 2, 3):
            grad_y[at * 3 + step - 1].wait_recv()
            grad = grad + grad_y_in[at * 3 + step - 1].astype(F32)
        for half in range(2):
            columns = slice(half * 128, half * 128 + 128)
            grad_own_slice[at * 2 + half] = grad[0:48, columns]
            for slot in range(4):
                grad_z_out[(at * 2 + half) * 4 + slot] = grad[slot * 48:slot * 48 + 48, columns].astype(BF)
    grad_z = [
        remote(
            grad_z_out.at[lax.rem(x + step, 4) * 4 + slot], grad_z_in.at[step * 4 + slot - 1], grad_z_sems, step * 4 + slot - 1,
            (feat_at(lax.rem(ring_at_me + TURN[slot], 4), cross_at_me), batch_at(step, 0)),
        )
        for step in range(4) for slot in range(4) if step + slot > 0
    ]
    for copy in grad_z:
        copy.start()
    grad = grad_own_slice[x]
    for at in range(15):
        grad_z[at].wait_recv()
        grad = grad + grad_z_in[at].astype(F32)
    pieces[piece] = grad
    spread = [remote(pieces.at[piece], pieces.at[piece], piece_sems, at, device) for at, device in enumerate(others)]
    for copy in spread:
        copy.start()
    for copy in spread:
        copy.wait_recv()
    for at in range(8):
        weight_grad[:, at * 128:at * 128 + 128] = pieces[at]
    for copy in ring + w_z + w_y + w_all + sum(all_sums, []) + relays + x_copies + grad_core + grad_y + grad_z + spread:
        copy.wait_send()


def per_device(features, sampled_slots, block_index, counts, weight, cotangent):
    hbm = pl.BlockSpec(memory_space=pl.ANY)
    vmem = pl.BlockSpec(memory_space=pltpu.VMEM)
    dma = pltpu.SemaphoreType.DMA
    return pl.pallas_call(
        layer_kernel,
        in_specs=[hbm] * 6,
        out_specs=(vmem, vmem),
        scratch_shapes=[
            pltpu.SMEM((8, 16, 32), jnp.int32),
            pltpu.VMEM((48, 16384), BF),
            pltpu.VMEM((128, 192, 128), BF),
            pltpu.VMEM((8, 16, 1024), jnp.int32),
            pltpu.VMEM((8, 8, 1024), jnp.int32),
            pltpu.VMEM((8, 256), jnp.int32),
            pltpu.VMEM((128, 128), jnp.int32),
            pltpu.VMEM((128, 128), jnp.int32),
            pltpu.VMEM((64, 8, 128, 256), BF),
            pltpu.VMEM((32, 192, 256), BF),
            pltpu.VMEM((32, 192, 256), BF),
            pltpu.VMEM((3, 768, 256), BF),
            pltpu.VMEM((2, 768, 256), BF),
            pltpu.VMEM((2, 384, 256), BF),
            pltpu.VMEM((8, 768, 128), BF),
            pltpu.VMEM((768, 256), BF),
            pltpu.VMEM((256, 768), BF),
            pltpu.VMEM((256, 1024), BF),
            pltpu.VMEM((2, 768, 256), F32),
            pltpu.VMEM((2, 768, 256), F32),
            pltpu.VMEM((6, 192, 256), BF),
            pltpu.VMEM((6, 192, 256), BF),
            pltpu.VMEM((2, 192, 256), F32),
            pltpu.VMEM((4, 48, 128), F32),
            pltpu.VMEM((16, 48, 128), BF),
            pltpu.VMEM((15, 48, 128), BF),
            pltpu.VMEM((8, 48, 128), F32),
            dma((13,)), dma((2, 6)), dma((2, 13)), dma((2, 28)), dma((2, 4)),
            dma((2, 2)), dma((2, 6)), dma((2, 15)), dma((2, 7)),
        ],
        out_shape=(
            jax.ShapeDtypeStruct((256, 1024), BF),
            jax.ShapeDtypeStruct((48, 1024), F32),
        ),
        compiler_params=pltpu.CompilerParams(vmem_limit_bytes=63 << 20, collective_id=0, has_side_effects=True),
    )(features, sampled_slots, counts, jnp.swapaxes(block_index, 2, 3), weight, cotangent)


def solution(mesh):
    placed = (
        P("feat", "batch"),
        P(None, "batch", None, None),
        P(None, "batch", None, None),
        P(),
        P("feat", None),
        P(("feat", "batch"), None),
    )
    return jax.shard_map(
        per_device,
        mesh=mesh,
        in_specs=placed,
        out_specs=(P(("feat", "batch"), None), P("feat", None)),
        check_vma=False,
    )
```

```python
import jax
import jax.numpy as jnp
from jax import lax
from jax.experimental import pallas as pl
from jax.experimental.pallas import tpu as pltpu
from jax.sharding import PartitionSpec as P

BF = jnp.bfloat16
F32 = jnp.float32
NT = (((1,), (1,)), ((), ()))


def edge_codes(slots, used):
    slot_row = lax.broadcasted_iota(jnp.int32, slots.shape, 0) & 15
    lane = lax.broadcasted_iota(jnp.int32, slots.shape, 1)
    height = slots.shape[0]
    value = jnp.where(slot_row < used, slots, -1)
    for bit in range(4):
        rows, lanes = 1 << bit, 8 << bit
        row_bit = (slot_row >> bit) & 1
        lane_bit = (lane >> (bit + 3)) & 1
        later = pltpu.roll(pltpu.roll(value, height - rows, 0), lanes, 1)
        earlier = pltpu.roll(pltpu.roll(value, rows, 0), 128 - lanes, 1)
        value = jnp.where(row_bit < lane_bit, later, jnp.where(row_bit > lane_bit, earlier, value))
    return (value >> 7) * 8 + (lane & 7), value & 127


def onehot(code):
    rows = lax.broadcasted_iota(jnp.int32, (128, 128), 0).astype(BF)
    match = jnp.broadcast_to(code.astype(BF), (128, 128)) == rows
    return jnp.where(match, BF(1), BF(0))


def build(adjacency, pairs_at, block, tile_codes, node_codes):
    blank = jnp.zeros((128, 128), BF)

    def diagonal(first, second):
        return jnp.concatenate([jnp.concatenate([first, blank], 1), jnp.concatenate([blank, second], 1)], 0)

    for pair in range(8):
        row = block * 16 + 2 * pair
        tile_a, tile_b = onehot(tile_codes[pl.ds(row, 1)]), onehot(tile_codes[pl.ds(row + 1, 1)])
        node_a, node_b = onehot(node_codes[pl.ds(row, 1)]), onehot(node_codes[pl.ds(row + 1, 1)])
        if pair % 2 == 0:
            left, right = jnp.concatenate([tile_a, tile_b], 1), diagonal(node_a, node_b)
        else:
            left, right = diagonal(tile_a, tile_b), jnp.concatenate([node_a, node_b], 1)
        both = lax.dot_general(left, right, NT, preferred_element_type=F32)
        both_a, both_b = (both[:, :128], both[:, 128:]) if pair % 2 == 0 else (both[:128], both[128:])
        rows = jnp.concatenate([both_a.reshape(16, 8, 128), both_b.reshape(16, 8, 128)], 1).astype(BF)
        for tile in range(16):
            adjacency[pairs_at, tile // 2, pair * 16:pair * 16 + 16, tile % 2 * 128:tile % 2 * 128 + 128] = rows[tile]


def remote(src, dst, sems, at, target):
    return pltpu.make_async_remote_copy(
        src_ref=src, dst_ref=dst, send_sem=sems.at[0, at], recv_sem=sems.at[1, at],
        device_id=target, device_id_type=pl.DeviceIdType.MESH,
    )


TURN = (0, 1, 3, 2)


def layer_kernel(
    features, slots, counts, block_index, weight, cotangent, hidden, weight_grad,
    tiles, raw, feats, slot_rows, used, own_used, tile_codes, node_codes, adjacency,
    sums_out, sums_in, x_out, x_in, relay_in, weights, rows, rows_t, cot,
    grad_out, grad_in, grad_y_out, grad_y_in, grad_own, grad_own_slice, grad_z_out, grad_z_in, pieces,
    load_sems, ring_sems, w_sems, sum_sems, x_sems, grad_core_sems, grad_y_sems, grad_z_sems, piece_sems,
):
    feat, batch = lax.axis_index("feat"), lax.axis_index("batch")
    z, y, x, core = feat // 4, feat % 4, batch // 2, batch % 2
    piece = core * 4 + x
    ring_at_me, cross_at_me = z + core * (y - z), y + core * (z - y)

    def feat_at(ring_place, cross_place):
        return ring_place * (4 - 3 * core) + cross_place * (1 + 3 * core)

    def batch_at(step, side):
        return lax.rem(x + step, 4) * 2 + lax.rem(core + side, 2)

    def ring_dev(step, side=0):
        return (feat_at(lax.rem(ring_at_me + step, 4), cross_at_me), batch_at(0, side))

    def cross_dev(step, side=0):
        return (feat_at(ring_at_me, lax.rem(cross_at_me + step, 4)), batch_at(0, side))

    def x_at(step, side=0):
        return (feat, batch_at(step, side))

    partner = x_at(0, 1)
    others = [x_at(step, side) for step in range(4) for side in range(2)][1:]
    barrier = pltpu.get_barrier_semaphore()
    greeted = [dev(step, side) for dev in (ring_dev, cross_dev) for side in range(2) for step in (1, 2, 3)] + others
    greeted += [
        (feat_at(lax.rem(ring_at_me + step, 4), cross_at_me), batch_at(x_step, 0)) for step in (1, 2, 3) for x_step in (1, 2, 3)
    ]
    for device in greeted:
        pl.semaphore_signal(barrier, inc=1, device_id=device, device_id_type=pl.DeviceIdType.MESH)

    def owned(owner):
        return pl.ds(pl.multiple_of(owner * 256, 256), 256)

    piece_columns = pl.ds(pl.multiple_of(piece * 128, 128), 128)
    loads = [
        pltpu.make_async_copy(features, raw, load_sems.at[0]),
        pltpu.make_async_copy(weight.at[:, piece_columns], weights.at[piece, pl.ds(0, 48)], load_sems.at[1]),
        pltpu.make_async_copy(cotangent, cot, load_sems.at[2]),
        pltpu.make_async_copy(counts.at[batch, :, owned(feat)], own_used, load_sems.at[3]),
        pltpu.make_async_copy(block_index.at[:, 0], tiles, load_sems.at[12]),
    ]
    for at in range(4):
        source, target = owned(feat_at(ring_at_me, at)), pl.ds(at * 256, 256)
        loads.append(pltpu.make_async_copy(slots.at[:, 0, :, source], slot_rows.at[:, :, target], load_sems.at[4 + 2 * at]))
        loads.append(pltpu.make_async_copy(counts.at[:, :, source], used.at[:, :, target], load_sems.at[5 + 2 * at]))
    for load in loads:
        load.start()
    loads[0].wait()
    for tile in range(128):
        feats[tile, 0:48, :] = raw[:, tile * 128:tile * 128 + 128]
    loads[1].wait()
    pl.semaphore_wait(barrier, len(greeted))

    low, high = pl.ds(0, 64), pl.ds(64, 64)

    def shard(at, part):
        return feats.at[part, pl.ds(48 * at, 48), :]

    ring = [
        remote(shard(0, low), shard(2, low), ring_sems, 0, ring_dev(1)),
        remote(shard(0, high), shard(1, high), ring_sems, 1, ring_dev(3)),
        remote(shard(0, high), shard(2, high), ring_sems, 2, ring_dev(1)),
        remote(shard(0, low), shard(1, low), ring_sems, 3, ring_dev(3)),
        remote(shard(2, low), shard(3, low), ring_sems, 4, ring_dev(1)),
        remote(shard(1, high), shard(3, high), ring_sems, 5, ring_dev(3)),
    ]

    mine = weights.at[piece]
    w_first = mine.at[pl.ds(0, 48)]
    w_z = [
        remote(w_first, mine.at[pl.ds(48 * {1: 2, 2: 3, 3: 1}[step], 48)], w_sems, step - 1, ring_dev(step))
        for step in (1, 2, 3)
    ]
    w_y = [
        remote(mine.at[pl.ds(0, 192)], mine.at[pl.ds(192 * (4 - step), 192)], w_sems, 2 + step, cross_dev(step))
        for step in (1, 2, 3)
    ]
    w_all = [
        remote(mine, mine, w_sems, 6 + at, device) for at, device in enumerate(others)
    ]
    for copy in w_z:
        copy.start()
    ring[0].start()
    ring[1].start()
    for load in loads[4:]:
        load.wait()

    def group_at(step):
        turn = step // 2
        side = 1 - step % 2
        owner_core = core + side * (1 - 2 * core)
        away = turn + 2 - (turn // 2) * (2 * turn - 1) + turn * (3 - turn) // 2 * (2 * turn - 3) * 2 * owner_core
        return batch_at(away, side)

    def build_group(step, unused):
        group = group_at(step)
        group_used = used[group, pl.ds(batch, 1), :]
        tile_code, node_code = edge_codes(
            jnp.concatenate([slot_rows[group, :, b * 128:b * 128 + 128] for b in range(8)], 0),
            jnp.concatenate([jnp.broadcast_to(group_used[:, b * 128:b * 128 + 128], (16, 128)) for b in range(8)], 0),
        )
        tile_codes[...] = tile_code
        node_codes[...] = node_code

        def some(turn, unused):
            for at in range(4):
                build(adjacency, step * 8 + turn * 4 + at, turn * 4 + at, tile_codes, node_codes)
            return 0

        return lax.fori_loop(0, 2, some, 0)

    lax.fori_loop(0, 2, build_group, 0)
    ring[2].start()
    ring[3].start()
    for copy in w_z:
        copy.wait_recv()
    for copy in w_y:
        copy.start()
    lax.fori_loop(2, 5, build_group, 0)
    ring[0].wait_recv()
    ring[1].wait_recv()
    ring[4].start()
    ring[5].start()
    for copy in w_y:
        copy.wait_recv()
    for copy in w_all:
        copy.start()
    lax.fori_loop(5, 8, build_group, 0)
    for at in (2, 3, 4, 5):
        ring[at].wait_recv()

    def products(step):
        group = group_at(step)

        def some(turn, unused):
            for at in range(4):
                owner = turn * 2 + at // 2
                block = feat_at(ring_at_me, owner) * 2 + at % 2
                total = jnp.zeros((192, 128), F32)
                for pair in range(8):
                    halves = [feats[tiles[group, pair * 2 + half, block]] for half in range(2)]
                    total += lax.dot_general(
                        jnp.concatenate(halves, 1),
                        adjacency[step * 8 + turn * 4 + at, pair],
                        NT,
                        preferred_element_type=F32,
                    )
                sums_out[step * 4 + owner, :, at % 2 * 128:at % 2 * 128 + 128] = total.astype(BF)
            return 0

        lax.fori_loop(0, 2, some, 0)

    def sum_copies(turn, side):
        copies = []
        for step in range(1 - side, 4):
            copies.append(
                remote(
                    sums_out.at[(turn * 2 + 1 - side) * 4 + lax.rem(cross_at_me + step, 4)],
                    sums_in.at[turn * 8 + side * 4 + (4 - step) % 4],
                    sum_sems, turn * 7 + side * 3 + step - 1 + side, cross_dev(step, side),
                )
            )
        return copies

    def owner_sum(turn, across):
        first = sums_out[(turn * 2 + 1) * 4 + cross_at_me] if across == 0 else sums_in[turn * 8 + across]
        second = [
            sums_in[turn * 8 + 4 + TURN[slot], TURN[across] * 48:TURN[across] * 48 + 48, :] for slot in range(4)
        ]
        return first.astype(F32) + jnp.concatenate(second, 0).astype(F32)

    x_second, x_third = 3 - 2 * core, 1 + 2 * core
    relays = [
        remote(x_out.at[0, pl.ds(384 * at, 384)], relay_in.at[at], x_sems, at, x_at((x_third, x_second)[at])) for at in range(2)
    ]
    x_copies = [remote(x_out.at[1 + at], x_in.at[at], x_sems, 2 + at, x_at((x_second, x_third)[at])) for at in range(2)]
    all_sums = []

    def finish(turn):
        for copy in all_sums[turn]:
            copy.wait_recv()
        if turn == 3:
            return
        if turn > 0:
            relays[2 - turn].wait_recv()
        for across in range(4):
            total = owner_sum(turn, across)
            if turn > 0 and across // 2 == 2 - turn:
                total = total + relay_in[across // 2, across % 2 * 192:across % 2 * 192 + 192, :].astype(F32)
            x_out[turn, across * 192:across * 192 + 192, :] = total.astype(BF)
        for copy in relays if turn == 0 else [x_copies[turn - 1]]:
            copy.start()

    for turn in range(4):
        copies = []
        for side in (1, 0):
            products(turn * 2 + 1 - side)
            new = sum_copies(turn, side)
            for copy in new:
                copy.start()
            copies += new
            if side == 1 and turn > 0:
                finish(turn - 1)
        all_sums.append(copies)
    loads[2].wait()
    loads[3].wait()
    for copy in w_all:
        copy.wait_recv()
    totals = jnp.sum(own_used[...], axis=0, keepdims=True).astype(F32)
    finish(3)
    for copy in x_copies:
        copy.wait_recv()
    for across in range(4):
        part = slice(across * 192, across * 192 + 192)
        summed = owner_sum(3, across)
        for turn in range(2):
            summed = summed + x_in[turn, part, :].astype(F32)
        rows[part, :] = (summed / totals).astype(BF)
    rows_t[...] = rows[...].T

    def swapped(part):
        return jnp.concatenate(
            [part[TURN[slot] * 192 + TURN[across] * 48:TURN[slot] * 192 + TURN[across] * 48 + 48]
             for across in range(4) for slot in range(4)],
            0,
        )

    def layer(tile, partners):
        columns = pl.ds(pl.multiple_of(tile * 256, 256), 256)
        part = jnp.concatenate([weights[tile * 2], weights[tile * 2 + 1]], 1)
        preact = jnp.dot(rows_t[...], swapped(part) if partners else part, preferred_element_type=F32)
        sigmoid_val = jax.nn.sigmoid(preact)
        hidden[:, columns] = (preact * sigmoid_val).astype(BF)
        pre_grad = cot[:, columns].astype(F32) * sigmoid_val * (1.0 + preact * (1.0 - sigmoid_val))
        return jnp.dot(rows[...], pre_grad.astype(BF), preferred_element_type=F32)

    halves = (slice(0, 128), slice(128, 256))
    grad_core = [remote(grad_out.at[at], grad_in.at[at], grad_core_sems, at, partner) for at in range(4)]
    for at in range(2):
        grad = layer((1 - core) * 2 + at, True)
        for half in range(2):
            grad_out[at * 2 + half] = grad[:, halves[half]]
            grad_core[at * 2 + half].start()
    grad_y = []
    for at in range(2):
        own_grad = layer(core * 2 + at, False)
        for half in range(2):
            part = at * 2 + half
            grad_core[part].wait_recv()
            grad = own_grad[:, halves[half]] + swapped(grad_in[part])
            grad_own[part] = grad[0:192]
            for step in (1, 2, 3):
                slot = part * 3 + step - 1
                grad_y_out[slot] = grad[step * 192:step * 192 + 192].astype(BF)
                grad_y.append(remote(grad_y_out.at[slot], grad_y_in.at[slot], grad_y_sems, slot, cross_dev(step)))
                grad_y[slot].start()
    for part in range(4):
        grad = grad_own[part]
        for step in (1, 2, 3):
            grad_y[part * 3 + step - 1].wait_recv()
            grad = grad + grad_y_in[part * 3 + step - 1].astype(F32)
        grad_own_slice[part] = grad[0:48]
        for slot in range(4):
            grad_z_out[part * 4 + slot] = grad[slot * 48:slot * 48 + 48].astype(BF)
    grad_z = [
        remote(
            grad_z_out.at[lax.rem(x + step, 4) * 4 + slot], grad_z_in.at[step * 4 + slot - 1], grad_z_sems, step * 4 + slot - 1,
            (feat_at(lax.rem(ring_at_me + TURN[slot], 4), cross_at_me), batch_at(step, 0)),
        )
        for step in range(4) for slot in range(4) if step + slot > 0
    ]
    for copy in grad_z:
        copy.start()
    grad = grad_own_slice[x]
    for at in range(15):
        grad_z[at].wait_recv()
        grad = grad + grad_z_in[at].astype(F32)
    pieces[piece] = grad
    spread = [remote(pieces.at[piece], pieces.at[piece], piece_sems, at, device) for at, device in enumerate(others)]
    for copy in spread:
        copy.start()
    for copy in spread:
        copy.wait_recv()
    for at in range(8):
        weight_grad[:, at * 128:at * 128 + 128] = pieces[at]
    for copy in ring + w_z + w_y + w_all + sum(all_sums, []) + relays + x_copies + grad_core + grad_y + grad_z + spread:
        copy.wait_send()


def per_device(features, sampled_slots, block_index, counts, weight, cotangent):
    hbm = pl.BlockSpec(memory_space=pl.ANY)
    vmem = pl.BlockSpec(memory_space=pltpu.VMEM)
    dma = pltpu.SemaphoreType.DMA
    return pl.pallas_call(
        layer_kernel,
        in_specs=[hbm] * 6,
        out_specs=(vmem, vmem),
        scratch_shapes=[
            pltpu.SMEM((8, 16, 32), jnp.int32),
            pltpu.VMEM((48, 16384), BF),
            pltpu.VMEM((128, 192, 128), BF),
            pltpu.VMEM((8, 16, 1024), jnp.int32),
            pltpu.VMEM((8, 8, 1024), jnp.int32),
            pltpu.VMEM((8, 256), jnp.int32),
            pltpu.VMEM((128, 128), jnp.int32),
            pltpu.VMEM((128, 128), jnp.int32),
            pltpu.VMEM((64, 8, 128, 256), BF),
            pltpu.VMEM((32, 192, 256), BF),
            pltpu.VMEM((32, 192, 256), BF),
            pltpu.VMEM((3, 768, 256), BF),
            pltpu.VMEM((2, 768, 256), BF),
            pltpu.VMEM((2, 384, 256), BF),
            pltpu.VMEM((8, 768, 128), BF),
            pltpu.VMEM((768, 256), BF),
            pltpu.VMEM((256, 768), BF),
            pltpu.VMEM((256, 1024), BF),
            pltpu.VMEM((4, 768, 128), F32),
            pltpu.VMEM((4, 768, 128), F32),
            pltpu.VMEM((12, 192, 128), BF),
            pltpu.VMEM((12, 192, 128), BF),
            pltpu.VMEM((4, 192, 128), F32),
            pltpu.VMEM((4, 48, 128), F32),
            pltpu.VMEM((16, 48, 128), BF),
            pltpu.VMEM((15, 48, 128), BF),
            pltpu.VMEM((8, 48, 128), F32),
            dma((13,)), dma((2, 6)), dma((2, 13)), dma((2, 28)), dma((2, 4)),
            dma((2, 4)), dma((2, 12)), dma((2, 15)), dma((2, 7)),
        ],
        out_shape=(
            jax.ShapeDtypeStruct((256, 1024), BF),
            jax.ShapeDtypeStruct((48, 1024), F32),
        ),
        compiler_params=pltpu.CompilerParams(vmem_limit_bytes=63 << 20, collective_id=0, has_side_effects=True),
    )(features, sampled_slots, counts, jnp.swapaxes(block_index, 2, 3), weight, cotangent)


def solution(mesh):
    placed = (
        P("feat", "batch"),
        P(None, "batch", None, None),
        P(None, "batch", None, None),
        P(),
        P("feat", None),
        P(("feat", "batch"), None),
    )
    return jax.shard_map(
        per_device,
        mesh=mesh,
        in_specs=placed,
        out_specs=(P(("feat", "batch"), None), P("feat", None)),
        check_vma=False,
    )
```

```python
import jax
import jax.numpy as jnp
from jax import lax
from jax.experimental import pallas as pl
from jax.experimental.pallas import tpu as pltpu
from jax.sharding import PartitionSpec as P

BF = jnp.bfloat16
F32 = jnp.float32
NT = (((1,), (1,)), ((), ()))


def edge_codes(slots, used):
    slot_row = lax.broadcasted_iota(jnp.int32, slots.shape, 0) & 15
    lane = lax.broadcasted_iota(jnp.int32, slots.shape, 1)
    height = slots.shape[0]
    value = jnp.where(slot_row < used, slots, -1)
    for bit in range(4):
        rows, lanes = 1 << bit, 8 << bit
        row_bit = (slot_row >> bit) & 1
        lane_bit = (lane >> (bit + 3)) & 1
        later = pltpu.roll(pltpu.roll(value, height - rows, 0), lanes, 1)
        earlier = pltpu.roll(pltpu.roll(value, rows, 0), 128 - lanes, 1)
        value = jnp.where(row_bit < lane_bit, later, jnp.where(row_bit > lane_bit, earlier, value))
    return (value >> 7) * 8 + (lane & 7), value & 127


def onehot(code):
    rows = lax.broadcasted_iota(jnp.int32, (128, 128), 0).astype(BF)
    match = jnp.broadcast_to(code.astype(BF), (128, 128)) == rows
    return jnp.where(match, BF(1), BF(0))


def build(adjacency, pairs_at, block, tile_codes, node_codes):
    blank = jnp.zeros((128, 128), BF)

    def diagonal(first, second):
        return jnp.concatenate([jnp.concatenate([first, blank], 1), jnp.concatenate([blank, second], 1)], 0)

    for pair in range(8):
        row = block * 16 + 2 * pair
        tile_a, tile_b = onehot(tile_codes[pl.ds(row, 1)]), onehot(tile_codes[pl.ds(row + 1, 1)])
        node_a, node_b = onehot(node_codes[pl.ds(row, 1)]), onehot(node_codes[pl.ds(row + 1, 1)])
        if pair % 2 == 0:
            left, right = jnp.concatenate([tile_a, tile_b], 1), diagonal(node_a, node_b)
        else:
            left, right = diagonal(tile_a, tile_b), jnp.concatenate([node_a, node_b], 1)
        both = lax.dot_general(left, right, NT, preferred_element_type=F32)
        both_a, both_b = (both[:, :128], both[:, 128:]) if pair % 2 == 0 else (both[:128], both[128:])
        rows = jnp.concatenate([both_a.reshape(16, 8, 128), both_b.reshape(16, 8, 128)], 1).astype(BF)
        for tile in range(16):
            adjacency[pairs_at, tile // 2, pair * 16:pair * 16 + 16, tile % 2 * 128:tile % 2 * 128 + 128] = rows[tile]


def remote(src, dst, sems, at, target):
    return pltpu.make_async_remote_copy(
        src_ref=src, dst_ref=dst, send_sem=sems.at[0, at], recv_sem=sems.at[1, at],
        device_id=target, device_id_type=pl.DeviceIdType.MESH,
    )


TURN = (0, 1, 3, 2)


def layer_kernel(
    features, slots, counts, block_index, weight, cotangent, hidden, weight_grad,
    tiles, raw, feats, slot_rows, used, own_used, tile_codes, node_codes, adjacency,
    sums_out, sums_in, x_out, x_in, relay_in, weights, rows, rows_t, cot,
    grad_out, grad_in, grad_y_out, grad_y_in, grad_own, grad_own_slice, grad_z_out, grad_z_in, pieces,
    load_sems, ring_sems, w_sems, sum_sems, x_sems, grad_core_sems, grad_y_sems, grad_z_sems, piece_sems,
):
    feat, batch = lax.axis_index("feat"), lax.axis_index("batch")
    z, y, x, core = feat // 4, feat % 4, batch // 2, batch % 2
    piece = core * 4 + x
    ring_at_me, cross_at_me = z + core * (y - z), y + core * (z - y)

    def feat_at(ring_place, cross_place):
        return ring_place * (4 - 3 * core) + cross_place * (1 + 3 * core)

    def batch_at(step, side):
        return lax.rem(x + step, 4) * 2 + lax.rem(core + side, 2)

    def ring_dev(step, side=0):
        return (feat_at(lax.rem(ring_at_me + step, 4), cross_at_me), batch_at(0, side))

    def cross_dev(step, side=0):
        return (feat_at(ring_at_me, lax.rem(cross_at_me + step, 4)), batch_at(0, side))

    def x_at(step, side=0):
        return (feat, batch_at(step, side))

    partner = x_at(0, 1)
    others = [x_at(step, side) for step in range(4) for side in range(2)][1:]
    barrier = pltpu.get_barrier_semaphore()
    greeted = [dev(step, side) for dev in (ring_dev, cross_dev) for side in range(2) for step in (1, 2, 3)] + others
    greeted += [
        (feat_at(lax.rem(ring_at_me + step, 4), cross_at_me), batch_at(x_step, 0)) for step in (1, 2, 3) for x_step in (1, 2, 3)
    ]
    for device in greeted:
        pl.semaphore_signal(barrier, inc=1, device_id=device, device_id_type=pl.DeviceIdType.MESH)

    def owned(owner):
        return pl.ds(pl.multiple_of(owner * 256, 256), 256)

    piece_columns = pl.ds(pl.multiple_of(piece * 128, 128), 128)
    loads = [
        pltpu.make_async_copy(features, raw, load_sems.at[0]),
        pltpu.make_async_copy(weight.at[:, piece_columns], weights.at[piece, pl.ds(0, 48)], load_sems.at[1]),
        pltpu.make_async_copy(cotangent, cot, load_sems.at[2]),
        pltpu.make_async_copy(counts.at[batch, :, owned(feat)], own_used, load_sems.at[3]),
        pltpu.make_async_copy(block_index.at[:, 0], tiles, load_sems.at[12]),
    ]
    for at in range(4):
        source, target = owned(feat_at(ring_at_me, at)), pl.ds(at * 256, 256)
        loads.append(pltpu.make_async_copy(slots.at[:, 0, :, source], slot_rows.at[:, :, target], load_sems.at[4 + 2 * at]))
        loads.append(pltpu.make_async_copy(counts.at[:, :, source], used.at[:, :, target], load_sems.at[5 + 2 * at]))
    for load in loads:
        load.start()
    loads[0].wait()
    for tile in range(128):
        feats[tile, 0:48, :] = raw[:, tile * 128:tile * 128 + 128]
    loads[1].wait()
    pl.semaphore_wait(barrier, len(greeted))

    low, high = pl.ds(0, 64), pl.ds(64, 64)

    def shard(at, part):
        return feats.at[part, pl.ds(48 * at, 48), :]

    ring = [
        remote(shard(0, low), shard(2, low), ring_sems, 0, ring_dev(1)),
        remote(shard(0, high), shard(1, high), ring_sems, 1, ring_dev(3)),
        remote(shard(0, high), shard(2, high), ring_sems, 2, ring_dev(1)),
        remote(shard(0, low), shard(1, low), ring_sems, 3, ring_dev(3)),
        remote(shard(2, low), shard(3, low), ring_sems, 4, ring_dev(1)),
        remote(shard(1, high), shard(3, high), ring_sems, 5, ring_dev(3)),
    ]

    mine = weights.at[piece]
    w_first = mine.at[pl.ds(0, 48)]
    w_z = [
        remote(w_first, mine.at[pl.ds(48 * {1: 2, 2: 3, 3: 1}[step], 48)], w_sems, step - 1, ring_dev(step))
        for step in (1, 2, 3)
    ]
    w_y = [
        remote(mine.at[pl.ds(0, 192)], mine.at[pl.ds(192 * (4 - step), 192)], w_sems, 2 + step, cross_dev(step))
        for step in (1, 2, 3)
    ]
    w_all = [
        remote(mine, mine, w_sems, 6 + at, device) for at, device in enumerate(others)
    ]
    for copy in w_z:
        copy.start()
    ring[0].start()
    ring[1].start()
    for load in loads[4:]:
        load.wait()

    def group_at(step):
        turn = step // 2
        side = 1 - step % 2
        owner_core = core + side * (1 - 2 * core)
        away = turn + 2 - (turn // 2) * (2 * turn - 1) + turn * (3 - turn) // 2 * (2 * turn - 3) * 2 * owner_core
        return batch_at(away, side)

    def build_group(step, unused):
        group = group_at(step)
        group_used = used[group, pl.ds(batch, 1), :]
        tile_code, node_code = edge_codes(
            jnp.concatenate([slot_rows[group, :, b * 128:b * 128 + 128] for b in range(8)], 0),
            jnp.concatenate([jnp.broadcast_to(group_used[:, b * 128:b * 128 + 128], (16, 128)) for b in range(8)], 0),
        )
        tile_codes[...] = tile_code
        node_codes[...] = node_code

        def some(turn, unused):
            for at in range(4):
                build(adjacency, step * 8 + turn * 4 + at, turn * 4 + at, tile_codes, node_codes)
            return 0

        return lax.fori_loop(0, 2, some, 0)

    lax.fori_loop(0, 2, build_group, 0)
    ring[2].start()
    ring[3].start()
    for copy in w_z:
        copy.wait_recv()
    for copy in w_y:
        copy.start()
    lax.fori_loop(2, 5, build_group, 0)
    ring[0].wait_recv()
    ring[1].wait_recv()
    ring[4].start()
    ring[5].start()
    for copy in w_y:
        copy.wait_recv()
    for copy in w_all:
        copy.start()
    lax.fori_loop(5, 8, build_group, 0)
    for at in (2, 3, 4, 5):
        ring[at].wait_recv()

    def products(step):
        group = group_at(step)

        def some(turn, unused):
            for at in range(4):
                owner = turn * 2 + at // 2
                block = feat_at(ring_at_me, owner) * 2 + at % 2
                total = jnp.zeros((192, 128), F32)
                for pair in range(8):
                    halves = [feats[tiles[group, pair * 2 + half, block]] for half in range(2)]
                    total += lax.dot_general(
                        jnp.concatenate(halves, 1),
                        adjacency[step * 8 + turn * 4 + at, pair],
                        NT,
                        preferred_element_type=F32,
                    )
                sums_out[step * 4 + owner, :, at % 2 * 128:at % 2 * 128 + 128] = total.astype(BF)
            return 0

        lax.fori_loop(0, 2, some, 0)

    def sum_copies(turn, side):
        copies = []
        for step in range(1 - side, 4):
            copies.append(
                remote(
                    sums_out.at[(turn * 2 + 1 - side) * 4 + lax.rem(cross_at_me + step, 4)],
                    sums_in.at[turn * 8 + side * 4 + (4 - step) % 4],
                    sum_sems, turn * 7 + side * 3 + step - 1 + side, cross_dev(step, side),
                )
            )
        return copies

    def owner_sum(turn, across):
        first = sums_out[(turn * 2 + 1) * 4 + cross_at_me] if across == 0 else sums_in[turn * 8 + across]
        second = [
            sums_in[turn * 8 + 4 + TURN[slot], TURN[across] * 48:TURN[across] * 48 + 48, :] for slot in range(4)
        ]
        return first.astype(F32) + jnp.concatenate(second, 0).astype(F32)

    x_second, x_third = 3 - 2 * core, 1 + 2 * core
    relays = [
        remote(x_out.at[0, pl.ds(384 * at, 384)], relay_in.at[at], x_sems, at, x_at((x_third, x_second)[at])) for at in range(2)
    ]
    x_copies = [remote(x_out.at[1 + at], x_in.at[at], x_sems, 2 + at, x_at((x_second, x_third)[at])) for at in range(2)]
    all_sums = []

    def finish(turn):
        for copy in all_sums[turn]:
            copy.wait_recv()
        if turn == 3:
            return
        if turn > 0:
            relays[2 - turn].wait_recv()
        for across in range(4):
            total = owner_sum(turn, across)
            if turn > 0 and across // 2 == 2 - turn:
                total = total + relay_in[across // 2, across % 2 * 192:across % 2 * 192 + 192, :].astype(F32)
            x_out[turn, across * 192:across * 192 + 192, :] = total.astype(BF)
        for copy in relays if turn == 0 else [x_copies[turn - 1]]:
            copy.start()

    for turn in range(4):
        copies = []
        for side in (0, 1):
            products(turn * 2 + 1 - side)
            new = sum_copies(turn, side)
            for copy in new:
                copy.start()
            copies += new
            if side == 0 and turn > 0:
                finish(turn - 1)
        all_sums.append(copies)
    loads[2].wait()
    loads[3].wait()
    for copy in w_all:
        copy.wait_recv()
    totals = jnp.sum(own_used[...], axis=0, keepdims=True).astype(F32)
    finish(3)
    for copy in x_copies:
        copy.wait_recv()
    for across in range(4):
        part = slice(across * 192, across * 192 + 192)
        summed = owner_sum(3, across)
        for turn in range(2):
            summed = summed + x_in[turn, part, :].astype(F32)
        rows[part, :] = (summed / totals).astype(BF)
    rows_t[...] = rows[...].T

    def swapped(part):
        return jnp.concatenate(
            [part[TURN[slot] * 192 + TURN[across] * 48:TURN[slot] * 192 + TURN[across] * 48 + 48]
             for across in range(4) for slot in range(4)],
            0,
        )

    def layer(tile, partners):
        columns = pl.ds(pl.multiple_of(tile * 256, 256), 256)
        part = jnp.concatenate([weights[tile * 2], weights[tile * 2 + 1]], 1)
        preact = jnp.dot(rows_t[...], swapped(part) if partners else part, preferred_element_type=F32)
        sigmoid_val = jax.nn.sigmoid(preact)
        hidden[:, columns] = (preact * sigmoid_val).astype(BF)
        pre_grad = cot[:, columns].astype(F32) * sigmoid_val * (1.0 + preact * (1.0 - sigmoid_val))
        return jnp.dot(rows[...], pre_grad.astype(BF), preferred_element_type=F32)

    halves = (slice(0, 128), slice(128, 256))
    grad_core = [remote(grad_out.at[at], grad_in.at[at], grad_core_sems, at, partner) for at in range(4)]
    for at in range(2):
        grad = layer((1 - core) * 2 + at, True)
        for half in range(2):
            grad_out[at * 2 + half] = grad[:, halves[half]]
            grad_core[at * 2 + half].start()
    grad_y = []
    for at in range(2):
        own_grad = layer(core * 2 + at, False)
        for half in range(2):
            part = at * 2 + half
            grad_core[part].wait_recv()
            grad = own_grad[:, halves[half]] + swapped(grad_in[part])
            grad_own[part] = grad[0:192]
            for step in (1, 2, 3):
                slot = part * 3 + step - 1
                grad_y_out[slot] = grad[step * 192:step * 192 + 192].astype(BF)
                grad_y.append(remote(grad_y_out.at[slot], grad_y_in.at[slot], grad_y_sems, slot, cross_dev(step)))
                grad_y[slot].start()
    for part in range(4):
        grad = grad_own[part]
        for step in (1, 2, 3):
            grad_y[part * 3 + step - 1].wait_recv()
            grad = grad + grad_y_in[part * 3 + step - 1].astype(F32)
        grad_own_slice[part] = grad[0:48]
        for slot in range(4):
            grad_z_out[part * 4 + slot] = grad[slot * 48:slot * 48 + 48].astype(BF)
    grad_z = [
        remote(
            grad_z_out.at[lax.rem(x + step, 4) * 4 + slot], grad_z_in.at[step * 4 + slot - 1], grad_z_sems, step * 4 + slot - 1,
            (feat_at(lax.rem(ring_at_me + TURN[slot], 4), cross_at_me), batch_at(step, 0)),
        )
        for step in range(4) for slot in range(4) if step + slot > 0
    ]
    for copy in grad_z:
        copy.start()
    grad = grad_own_slice[x]
    for at in range(15):
        grad_z[at].wait_recv()
        grad = grad + grad_z_in[at].astype(F32)
    pieces[piece] = grad
    spread = [remote(pieces.at[piece], pieces.at[piece], piece_sems, at, device) for at, device in enumerate(others)]
    for copy in spread:
        copy.start()
    for copy in spread:
        copy.wait_recv()
    for at in range(8):
        weight_grad[:, at * 128:at * 128 + 128] = pieces[at]
    for copy in ring + w_z + w_y + w_all + sum(all_sums, []) + relays + x_copies + grad_core + grad_y + grad_z + spread:
        copy.wait_send()


def per_device(features, sampled_slots, block_index, counts, weight, cotangent):
    hbm = pl.BlockSpec(memory_space=pl.ANY)
    vmem = pl.BlockSpec(memory_space=pltpu.VMEM)
    dma = pltpu.SemaphoreType.DMA
    return pl.pallas_call(
        layer_kernel,
        in_specs=[hbm] * 6,
        out_specs=(vmem, vmem),
        scratch_shapes=[
            pltpu.SMEM((8, 16, 32), jnp.int32),
            pltpu.VMEM((48, 16384), BF),
            pltpu.VMEM((128, 192, 128), BF),
            pltpu.VMEM((8, 16, 1024), jnp.int32),
            pltpu.VMEM((8, 8, 1024), jnp.int32),
            pltpu.VMEM((8, 256), jnp.int32),
            pltpu.VMEM((128, 128), jnp.int32),
            pltpu.VMEM((128, 128), jnp.int32),
            pltpu.VMEM((64, 8, 128, 256), BF),
            pltpu.VMEM((32, 192, 256), BF),
            pltpu.VMEM((32, 192, 256), BF),
            pltpu.VMEM((3, 768, 256), BF),
            pltpu.VMEM((2, 768, 256), BF),
            pltpu.VMEM((2, 384, 256), BF),
            pltpu.VMEM((8, 768, 128), BF),
            pltpu.VMEM((768, 256), BF),
            pltpu.VMEM((256, 768), BF),
            pltpu.VMEM((256, 1024), BF),
            pltpu.VMEM((4, 768, 128), F32),
            pltpu.VMEM((4, 768, 128), F32),
            pltpu.VMEM((12, 192, 128), BF),
            pltpu.VMEM((12, 192, 128), BF),
            pltpu.VMEM((4, 192, 128), F32),
            pltpu.VMEM((4, 48, 128), F32),
            pltpu.VMEM((16, 48, 128), BF),
            pltpu.VMEM((15, 48, 128), BF),
            pltpu.VMEM((8, 48, 128), F32),
            dma((13,)), dma((2, 6)), dma((2, 13)), dma((2, 28)), dma((2, 4)),
            dma((2, 4)), dma((2, 12)), dma((2, 15)), dma((2, 7)),
        ],
        out_shape=(
            jax.ShapeDtypeStruct((256, 1024), BF),
            jax.ShapeDtypeStruct((48, 1024), F32),
        ),
        compiler_params=pltpu.CompilerParams(vmem_limit_bytes=63 << 20, collective_id=0, has_side_effects=True),
    )(features, sampled_slots, counts, jnp.swapaxes(block_index, 2, 3), weight, cotangent)


def solution(mesh):
    placed = (
        P("feat", "batch"),
        P(None, "batch", None, None),
        P(None, "batch", None, None),
        P(),
        P("feat", None),
        P(("feat", "batch"), None),
    )
    return jax.shard_map(
        per_device,
        mesh=mesh,
        in_specs=placed,
        out_specs=(P(("feat", "batch"), None), P("feat", None)),
        check_vma=False,
    )
```

```python
import jax
import jax.numpy as jnp
from jax import lax
from jax.experimental import pallas as pl
from jax.experimental.pallas import tpu as pltpu
from jax.sharding import PartitionSpec as P

BF = jnp.bfloat16
F32 = jnp.float32
NT = (((1,), (1,)), ((), ()))


def edge_codes(slots, used):
    slot_row = lax.broadcasted_iota(jnp.int32, slots.shape, 0) & 15
    lane = lax.broadcasted_iota(jnp.int32, slots.shape, 1)
    height = slots.shape[0]
    value = jnp.where(slot_row < used, slots, -1)
    for bit in range(4):
        rows, lanes = 1 << bit, 8 << bit
        row_bit = (slot_row >> bit) & 1
        lane_bit = (lane >> (bit + 3)) & 1
        later = pltpu.roll(pltpu.roll(value, height - rows, 0), lanes, 1)
        earlier = pltpu.roll(pltpu.roll(value, rows, 0), 128 - lanes, 1)
        value = jnp.where(row_bit < lane_bit, later, jnp.where(row_bit > lane_bit, earlier, value))
    return (value >> 7) * 8 + (lane & 7), value & 127


def onehot(code):
    rows = lax.broadcasted_iota(jnp.int32, (128, 128), 0).astype(BF)
    match = jnp.broadcast_to(code.astype(BF), (128, 128)) == rows
    return jnp.where(match, BF(1), BF(0))


def build(adjacency, pairs_at, block, tile_codes, node_codes):
    blank = jnp.zeros((128, 128), BF)

    def diagonal(first, second):
        return jnp.concatenate([jnp.concatenate([first, blank], 1), jnp.concatenate([blank, second], 1)], 0)

    for pair in range(8):
        row = block * 16 + 2 * pair
        tile_a, tile_b = onehot(tile_codes[pl.ds(row, 1)]), onehot(tile_codes[pl.ds(row + 1, 1)])
        node_a, node_b = onehot(node_codes[pl.ds(row, 1)]), onehot(node_codes[pl.ds(row + 1, 1)])
        if pair % 2 == 0:
            left, right = jnp.concatenate([tile_a, tile_b], 1), diagonal(node_a, node_b)
        else:
            left, right = diagonal(tile_a, tile_b), jnp.concatenate([node_a, node_b], 1)
        both = lax.dot_general(left, right, NT, preferred_element_type=F32)
        both_a, both_b = (both[:, :128], both[:, 128:]) if pair % 2 == 0 else (both[:128], both[128:])
        rows = jnp.concatenate([both_a.reshape(16, 8, 128), both_b.reshape(16, 8, 128)], 1).astype(BF)
        for tile in range(16):
            adjacency[pairs_at, tile // 2, pair * 16:pair * 16 + 16, tile % 2 * 128:tile % 2 * 128 + 128] = rows[tile]


def remote(src, dst, sems, at, target):
    return pltpu.make_async_remote_copy(
        src_ref=src, dst_ref=dst, send_sem=sems.at[0, at], recv_sem=sems.at[1, at],
        device_id=target, device_id_type=pl.DeviceIdType.MESH,
    )


TURN = (0, 1, 3, 2)


def layer_kernel(
    features, slots, counts, block_index, weight, cotangent, hidden, weight_grad,
    tiles, raw, feats, slot_rows, used, own_used, tile_codes, node_codes, adjacency,
    sums_out, sums_in, x_out, x_in, relay_in, weights, rows, rows_t, cot,
    grad_out, grad_in, grad_y_out, grad_y_in, grad_own, grad_own_slice, grad_z_out, grad_z_in, pieces,
    load_sems, ring_sems, w_sems, sum_sems, x_sems, grad_core_sems, grad_y_sems, grad_z_sems, piece_sems,
):
    feat, batch = lax.axis_index("feat"), lax.axis_index("batch")
    z, y, x, core = feat // 4, feat % 4, batch // 2, batch % 2
    piece = core * 4 + x
    ring_at_me, cross_at_me = z + core * (y - z), y + core * (z - y)

    def feat_at(ring_place, cross_place):
        return ring_place * (4 - 3 * core) + cross_place * (1 + 3 * core)

    def batch_at(step, side):
        return lax.rem(x + step, 4) * 2 + lax.rem(core + side, 2)

    def ring_dev(step, side=0):
        return (feat_at(lax.rem(ring_at_me + step, 4), cross_at_me), batch_at(0, side))

    def cross_dev(step, side=0):
        return (feat_at(ring_at_me, lax.rem(cross_at_me + step, 4)), batch_at(0, side))

    def x_at(step, side=0):
        return (feat, batch_at(step, side))

    partner = x_at(0, 1)
    others = [x_at(step, side) for step in range(4) for side in range(2)][1:]
    barrier = pltpu.get_barrier_semaphore()
    greeted = [dev(step, side) for dev in (ring_dev, cross_dev) for side in range(2) for step in (1, 2, 3)] + others
    greeted += [
        (feat_at(lax.rem(ring_at_me + step, 4), cross_at_me), batch_at(x_step, 0)) for step in (1, 2, 3) for x_step in (1, 2, 3)
    ]
    for device in greeted:
        pl.semaphore_signal(barrier, inc=1, device_id=device, device_id_type=pl.DeviceIdType.MESH)

    def owned(owner):
        return pl.ds(pl.multiple_of(owner * 256, 256), 256)

    piece_columns = pl.ds(pl.multiple_of(piece * 128, 128), 128)
    loads = [
        pltpu.make_async_copy(features, raw, load_sems.at[0]),
        pltpu.make_async_copy(weight.at[:, piece_columns], weights.at[piece, pl.ds(0, 48)], load_sems.at[1]),
        pltpu.make_async_copy(cotangent, cot, load_sems.at[2]),
        pltpu.make_async_copy(counts.at[batch, :, owned(feat)], own_used, load_sems.at[3]),
        pltpu.make_async_copy(block_index.at[:, 0], tiles, load_sems.at[12]),
    ]
    for at in range(4):
        source, target = owned(feat_at(ring_at_me, at)), pl.ds(at * 256, 256)
        loads.append(pltpu.make_async_copy(slots.at[:, 0, :, source], slot_rows.at[:, :, target], load_sems.at[4 + 2 * at]))
        loads.append(pltpu.make_async_copy(counts.at[:, :, source], used.at[:, :, target], load_sems.at[5 + 2 * at]))
    for load in loads:
        load.start()
    loads[0].wait()
    for tile in range(128):
        feats[tile, 0:48, :] = raw[:, tile * 128:tile * 128 + 128]
    loads[1].wait()
    pl.semaphore_wait(barrier, len(greeted))

    low, high = pl.ds(0, 64), pl.ds(64, 64)

    def shard(at, part):
        return feats.at[part, pl.ds(48 * at, 48), :]

    ring = [
        remote(shard(0, low), shard(2, low), ring_sems, 0, ring_dev(1)),
        remote(shard(0, high), shard(1, high), ring_sems, 1, ring_dev(3)),
        remote(shard(0, high), shard(2, high), ring_sems, 2, ring_dev(1)),
        remote(shard(0, low), shard(1, low), ring_sems, 3, ring_dev(3)),
        remote(shard(2, low), shard(3, low), ring_sems, 4, ring_dev(1)),
        remote(shard(1, high), shard(3, high), ring_sems, 5, ring_dev(3)),
    ]

    mine = weights.at[piece]
    w_first = mine.at[pl.ds(0, 48)]
    w_z = [
        remote(w_first, mine.at[pl.ds(48 * {1: 2, 2: 3, 3: 1}[step], 48)], w_sems, step - 1, ring_dev(step))
        for step in (1, 2, 3)
    ]
    w_y = [
        remote(mine.at[pl.ds(0, 192)], mine.at[pl.ds(192 * (4 - step), 192)], w_sems, 2 + step, cross_dev(step))
        for step in (1, 2, 3)
    ]
    w_all = [
        remote(mine, mine, w_sems, 6 + at, device) for at, device in enumerate(others)
    ]
    for copy in w_z:
        copy.start()
    ring[0].start()
    ring[1].start()
    for load in loads[4:]:
        load.wait()

    def group_at(step):
        turn = step // 2
        side = 1 - step % 2
        owner_core = core + side * (1 - 2 * core)
        away = turn + 2 - (turn // 2) * (2 * turn - 1) + turn * (3 - turn) // 2 * (2 * turn - 3) * 2 * owner_core
        return batch_at(away, side)

    def build_group(step, unused):
        group = group_at(step)
        group_used = used[group, pl.ds(batch, 1), :]
        tile_code, node_code = edge_codes(
            jnp.concatenate([slot_rows[group, :, b * 128:b * 128 + 128] for b in range(8)], 0),
            jnp.concatenate([jnp.broadcast_to(group_used[:, b * 128:b * 128 + 128], (16, 128)) for b in range(8)], 0),
        )
        tile_codes[...] = tile_code
        node_codes[...] = node_code

        def some(turn, unused):
            for at in range(4):
                build(adjacency, step * 8 + turn * 4 + at, turn * 4 + at, tile_codes, node_codes)
            return 0

        return lax.fori_loop(0, 2, some, 0)

    lax.fori_loop(0, 2, build_group, 0)
    ring[2].start()
    ring[3].start()
    for copy in w_z:
        copy.wait_recv()
    for copy in w_y:
        copy.start()
    lax.fori_loop(2, 4, build_group, 0)
    ring[0].wait_recv()
    ring[1].wait_recv()
    ring[4].start()
    ring[5].start()
    for copy in w_y:
        copy.wait_recv()
    for copy in w_all:
        copy.start()
    lax.fori_loop(4, 8, build_group, 0)
    for at in (2, 3, 4, 5):
        ring[at].wait_recv()

    def products(step):
        group = group_at(step)

        def some(turn, unused):
            for at in range(4):
                owner = turn * 2 + at // 2
                block = feat_at(ring_at_me, owner) * 2 + at % 2
                total = jnp.zeros((192, 128), F32)
                for pair in range(8):
                    halves = [feats[tiles[group, pair * 2 + half, block]] for half in range(2)]
                    total += lax.dot_general(
                        jnp.concatenate(halves, 1),
                        adjacency[step * 8 + turn * 4 + at, pair],
                        NT,
                        preferred_element_type=F32,
                    )
                sums_out[step * 4 + owner, :, at % 2 * 128:at % 2 * 128 + 128] = total.astype(BF)
            return 0

        lax.fori_loop(0, 2, some, 0)

    def sum_copies(turn, side):
        copies = []
        for step in range(1 - side, 4):
            copies.append(
                remote(
                    sums_out.at[(turn * 2 + 1 - side) * 4 + lax.rem(cross_at_me + step, 4)],
                    sums_in.at[turn * 8 + side * 4 + (4 - step) % 4],
                    sum_sems, turn * 7 + side * 3 + step - 1 + side, cross_dev(step, side),
                )
            )
        return copies

    def owner_sum(turn, across):
        first = sums_out[(turn * 2 + 1) * 4 + cross_at_me] if across == 0 else sums_in[turn * 8 + across]
        second = [
            sums_in[turn * 8 + 4 + TURN[slot], TURN[across] * 48:TURN[across] * 48 + 48, :] for slot in range(4)
        ]
        return first.astype(F32) + jnp.concatenate(second, 0).astype(F32)

    x_second, x_third = 3 - 2 * core, 1 + 2 * core
    relays = [
        remote(x_out.at[0, pl.ds(384 * at, 384)], relay_in.at[at], x_sems, at, x_at((x_third, x_second)[at])) for at in range(2)
    ]
    x_copies = [remote(x_out.at[1 + at], x_in.at[at], x_sems, 2 + at, x_at((x_second, x_third)[at])) for at in range(2)]
    all_sums = []

    def finish(turn):
        for copy in all_sums[turn]:
            copy.wait_recv()
        if turn == 3:
            return
        if turn > 0:
            relays[2 - turn].wait_recv()
        for across in range(4):
            total = owner_sum(turn, across)
            if turn > 0 and across // 2 == 2 - turn:
                total = total + relay_in[across // 2, across % 2 * 192:across % 2 * 192 + 192, :].astype(F32)
            x_out[turn, across * 192:across * 192 + 192, :] = total.astype(BF)
        for copy in relays if turn == 0 else [x_copies[turn - 1]]:
            copy.start()

    for turn in range(4):
        copies = []
        for side in (0, 1):
            products(turn * 2 + 1 - side)
            new = sum_copies(turn, side)
            for copy in new:
                copy.start()
            copies += new
            if side == 0 and turn > 0:
                finish(turn - 1)
        all_sums.append(copies)
    loads[2].wait()
    loads[3].wait()
    for copy in w_all:
        copy.wait_recv()
    totals = jnp.sum(own_used[...], axis=0, keepdims=True).astype(F32)
    finish(3)
    for copy in x_copies:
        copy.wait_recv()
    for across in range(4):
        part = slice(across * 192, across * 192 + 192)
        summed = owner_sum(3, across)
        for turn in range(2):
            summed = summed + x_in[turn, part, :].astype(F32)
        rows[part, :] = (summed / totals).astype(BF)
    rows_t[...] = rows[...].T

    def swapped(part):
        return jnp.concatenate(
            [part[TURN[slot] * 192 + TURN[across] * 48:TURN[slot] * 192 + TURN[across] * 48 + 48]
             for across in range(4) for slot in range(4)],
            0,
        )

    def layer(tile, partners):
        columns = pl.ds(pl.multiple_of(tile * 256, 256), 256)
        part = jnp.concatenate([weights[tile * 2], weights[tile * 2 + 1]], 1)
        preact = jnp.dot(rows_t[...], swapped(part) if partners else part, preferred_element_type=F32)
        sigmoid_val = jax.nn.sigmoid(preact)
        hidden[:, columns] = (preact * sigmoid_val).astype(BF)
        pre_grad = cot[:, columns].astype(F32) * sigmoid_val * (1.0 + preact * (1.0 - sigmoid_val))
        return jnp.dot(rows[...], pre_grad.astype(BF), preferred_element_type=F32)

    halves = (slice(0, 128), slice(128, 256))
    grad_core = [remote(grad_out.at[at], grad_in.at[at], grad_core_sems, at, partner) for at in range(4)]
    for at in range(2):
        grad = layer((1 - core) * 2 + at, True)
        for half in range(2):
            grad_out[at * 2 + half] = grad[:, halves[half]]
            grad_core[at * 2 + half].start()
    grad_y = []
    for at in range(2):
        own_grad = layer(core * 2 + at, False)
        for half in range(2):
            part = at * 2 + half
            grad_core[part].wait_recv()
            grad = own_grad[:, halves[half]] + swapped(grad_in[part])
            grad_own[part] = grad[0:192]
            for step in (1, 2, 3):
                slot = part * 3 + step - 1
                grad_y_out[slot] = grad[step * 192:step * 192 + 192].astype(BF)
                grad_y.append(remote(grad_y_out.at[slot], grad_y_in.at[slot], grad_y_sems, slot, cross_dev(step)))
                grad_y[slot].start()
    for part in range(4):
        grad = grad_own[part]
        for step in (1, 2, 3):
            grad_y[part * 3 + step - 1].wait_recv()
            grad = grad + grad_y_in[part * 3 + step - 1].astype(F32)
        grad_own_slice[part] = grad[0:48]
        for slot in range(4):
            grad_z_out[part * 4 + slot] = grad[slot * 48:slot * 48 + 48].astype(BF)
    grad_z = [
        remote(
            grad_z_out.at[lax.rem(x + step, 4) * 4 + slot], grad_z_in.at[step * 4 + slot - 1], grad_z_sems, step * 4 + slot - 1,
            (feat_at(lax.rem(ring_at_me + TURN[slot], 4), cross_at_me), batch_at(step, 0)),
        )
        for step in range(4) for slot in range(4) if step + slot > 0
    ]
    for copy in grad_z:
        copy.start()
    grad = grad_own_slice[x]
    for at in range(15):
        grad_z[at].wait_recv()
        grad = grad + grad_z_in[at].astype(F32)
    pieces[piece] = grad
    spread = [remote(pieces.at[piece], pieces.at[piece], piece_sems, at, device) for at, device in enumerate(others)]
    for copy in spread:
        copy.start()
    for copy in spread:
        copy.wait_recv()
    for at in range(8):
        weight_grad[:, at * 128:at * 128 + 128] = pieces[at]
    for copy in ring + w_z + w_y + w_all + sum(all_sums, []) + relays + x_copies + grad_core + grad_y + grad_z + spread:
        copy.wait_send()


def per_device(features, sampled_slots, block_index, counts, weight, cotangent):
    hbm = pl.BlockSpec(memory_space=pl.ANY)
    vmem = pl.BlockSpec(memory_space=pltpu.VMEM)
    dma = pltpu.SemaphoreType.DMA
    return pl.pallas_call(
        layer_kernel,
        in_specs=[hbm] * 6,
        out_specs=(vmem, vmem),
        scratch_shapes=[
            pltpu.SMEM((8, 16, 32), jnp.int32),
            pltpu.VMEM((48, 16384), BF),
            pltpu.VMEM((128, 192, 128), BF),
            pltpu.VMEM((8, 16, 1024), jnp.int32),
            pltpu.VMEM((8, 8, 1024), jnp.int32),
            pltpu.VMEM((8, 256), jnp.int32),
            pltpu.VMEM((128, 128), jnp.int32),
            pltpu.VMEM((128, 128), jnp.int32),
            pltpu.VMEM((64, 8, 128, 256), BF),
            pltpu.VMEM((32, 192, 256), BF),
            pltpu.VMEM((32, 192, 256), BF),
            pltpu.VMEM((3, 768, 256), BF),
            pltpu.VMEM((2, 768, 256), BF),
            pltpu.VMEM((2, 384, 256), BF),
            pltpu.VMEM((8, 768, 128), BF),
            pltpu.VMEM((768, 256), BF),
            pltpu.VMEM((256, 768), BF),
            pltpu.VMEM((256, 1024), BF),
            pltpu.VMEM((4, 768, 128), F32),
            pltpu.VMEM((4, 768, 128), F32),
            pltpu.VMEM((12, 192, 128), BF),
            pltpu.VMEM((12, 192, 128), BF),
            pltpu.VMEM((4, 192, 128), F32),
            pltpu.VMEM((4, 48, 128), F32),
            pltpu.VMEM((16, 48, 128), BF),
            pltpu.VMEM((15, 48, 128), BF),
            pltpu.VMEM((8, 48, 128), F32),
            dma((13,)), dma((2, 6)), dma((2, 13)), dma((2, 28)), dma((2, 4)),
            dma((2, 4)), dma((2, 12)), dma((2, 15)), dma((2, 7)),
        ],
        out_shape=(
            jax.ShapeDtypeStruct((256, 1024), BF),
            jax.ShapeDtypeStruct((48, 1024), F32),
        ),
        compiler_params=pltpu.CompilerParams(vmem_limit_bytes=63 << 20, collective_id=0, has_side_effects=True),
    )(features, sampled_slots, counts, jnp.swapaxes(block_index, 2, 3), weight, cotangent)


def solution(mesh):
    placed = (
        P("feat", "batch"),
        P(None, "batch", None, None),
        P(None, "batch", None, None),
        P(),
        P("feat", None),
        P(("feat", "batch"), None),
    )
    return jax.shard_map(
        per_device,
        mesh=mesh,
        in_specs=placed,
        out_specs=(P(("feat", "batch"), None), P("feat", None)),
        check_vma=False,
    )
```
